256 devices in a mesh: row: 32 (over y, x, core), col: 8 (over z).
Axes of the slice: x: 4, y: 4, z: 8, core: 2. Of those that a mesh axis runs over, the one named last changes fastest.
Arguments:
- cov: float32 [1, 32, 256, 4, 8, 256], P(None, 'row', None, None, 'col'), may hold values from -0.4 to 48, as said below
- noise: float32 [], replicated, may hold values from 0.5 to 2
Outputs:
- factor: float32 [1, 32, 256, 2, 256], P(None, 'row')
- trailing: float32 [1, 32, 256, 4, 8, 256], P(None, 'row', None, None, 'col')
The draws below stay inside these ranges and needn't reach their ends.
Inputs may be any that keep to these rules, and one draw needn't show every extreme that they name: cov is symmetric and A0 is positive definite; its Schur complements after one and two panels stay positive definite.
All inputs are finite; a program needn't handle non-finite values.
Results may differ from the reference program's by a relative error of at most 0.00017.
Values sent between devices are 32-bit elements; how exact they have to be, the bound alone decides.
A program may use at most 64 MiB of HBM per device.

```python
import math
import jax
import jax.numpy as jnp
from jax import lax

NB = 256
KR = 1
M = 8192
KC = 4
N_ROW = 32
N_COL = 8


def draw_cov(key, part):
    key = jax.random.fold_in(key, 11)
    base_key, head_key, tail_key, amp_key = jax.random.split(key, 4)
    base = jax.random.truncated_normal(base_key, -4.0, 4.0, (M, M), jnp.float32)
    index = jnp.arange(M)
    head = index < 2 * NB
    cross = head[:, None] != head[None, :]
    scale = jnp.where(cross, jnp.sqrt(60.0 / M), 1.0 / jnp.sqrt(1.0 * M)).astype(jnp.float32)
    sym = jnp.clip((base + base.T) * 0.5 * scale, -0.4, 0.4)
    head_diag = jnp.exp(jax.random.uniform(head_key, (M,), jnp.float32, jnp.log(3.0), jnp.log(6.0)))
    tail_diag = jnp.exp(jax.random.uniform(tail_key, (M,), jnp.float32, jnp.log(24.0), jnp.log(48.0)))
    diag_values = jnp.where(head, head_diag, tail_diag)
    sym = jnp.where(index[:, None] == index[None, :], diag_values[:, None], sym)
    head_index = jnp.arange(2 * NB)
    amplitude = jnp.exp(jax.random.uniform(amp_key, (2 * NB,), jnp.float32, jnp.log(0.7), jnp.log(1.4)))
    distance = jnp.abs(head_index[:, None] - head_index[None, :]).astype(jnp.float32)
    kernel = amplitude[:, None] * amplitude[None, :] * jnp.exp(-distance / 8.0)
    kernel = jnp.pad(kernel, ((0, M - 2 * NB), (0, M - 2 * NB)))
    sym = sym + kernel
    return sym.reshape(KR, N_ROW, NB, KC, N_COL, NB).astype(jnp.float32)


def setup_inputs(seed: int = 0) -> dict:
    splits = jax.random.split(jax.random.key(seed), 3)
    cov = draw_cov(jax.random.fold_in(splits[2], 71), 0)
    noise = jnp.clip(jnp.exp(jax.random.uniform(splits[1], (), jnp.float32, math.log(0.5), math.log(2.0))), 0.5, 2.0)
    return {"cov": cov, "noise": noise}


def reference(cov, noise):
    mat = cov.reshape(M, M) + noise * jnp.eye(M, dtype=jnp.float32)
    tile_of = (jnp.arange(M) // NB).astype(jnp.int32)
    panels = []
    for k in range(2):
        start = k * NB
        column = mat[:, start:start + NB]
        lower = jnp.linalg.cholesky(column[start:start + NB])
        solved = lax.linalg.triangular_solve(lower, column, left_side=False, lower=True, transpose_a=True)
        stacked = jnp.tile(lower, (M // NB, 1))
        panel = jnp.where(tile_of[:, None] < k, jnp.float32(0.0), jnp.where(tile_of[:, None] == k, stacked, solved))
        mat = mat - jnp.dot(panel, panel.T, precision=lax.Precision.HIGHEST)
        panels.append(panel)
    keep = (tile_of[:, None] >= 2) & (tile_of[None, :] >= 2)
    trailing = jnp.where(keep, mat, jnp.float32(0.0)).reshape(KR, N_ROW, NB, KC, N_COL, NB)
    factor = jnp.stack(panels, axis=1).reshape(KR, N_ROW, NB, 2, NB)
    return (factor, trailing)
```

```python
import jax
import jax.numpy as jnp
from jax import lax
from jax.experimental import pallas as pl
from jax.experimental.pallas import tpu as pltpu
from jax.sharding import PartitionSpec as P

F32 = jnp.float32
HIGHEST = lax.Precision.HIGHEST
NN = ((1,), (0,))
TN = ((0,), (0,))
NT = ((1,), (1,))
MESH = pl.DeviceIdType.MESH
CHUNKS = 2
WIDTHS = (512, 384, 256, 128)


def dot(a, b, dims):
    return lax.dot_general(a, b, (dims, ((), ())), precision=HIGHEST, preferred_element_type=F32)


def lanes(v, q):
    return jnp.broadcast_to(v[:, q : q + 1], (8, 128))


def sublanes(v, j):
    return jnp.broadcast_to(v[j : j + 1, :], (8, 128))


def factor_inverse_64(tile, group=16):
    count = 8
    per = group // 8
    sub = lax.broadcasted_iota(jnp.int32, (8, 128), 0)
    lane = lax.broadcasted_iota(jnp.int32, (8, 128), 1)
    rows = []
    for h in range(count):
        left = jnp.concatenate([tile[8 * h : 8 * h + 8, :], jnp.zeros((8, 64), F32)], axis=1)
        rows.append(jnp.where(lane < 64, left, (lane - 64 == sub + 8 * h).astype(F32)))
    out = [None] * count
    for g in range(64 // group):
        first = g * per
        col = [[lanes(rows[first + a], group * g + j) for a in range(per)] for j in range(group)]
        later = range(first + per, count)
        mult = {h: [lanes(rows[h], group * g + j) for j in range(group)] for h in later}
        z = [rows[first + a] for a in range(per)]
        w = [jnp.zeros((8, 128), F32) for _ in range(per)]
        pivot = sublanes(col[0][0], 0)
        for j in range(group):
            a0, s0 = j // 8, j % 8
            here = sub == s0
            inv = 1.0 / pivot
            root = lax.rsqrt(pivot)
            if j + 1 < group:
                a1, s1 = (j + 1) // 8, (j + 1) % 8
                cross = sublanes(col[j][a1], s1) * sublanes(col[j + 1][a0], s0)
                pivot = sublanes(col[j + 1][a1], s1) - cross * inv
            line = sublanes(z[a0], s0)
            w[a0] = jnp.where(here, line * root, w[a0])
            line = line * inv
            for a in range(per):
                t = z[a] - col[j][a] * line
                z[a] = jnp.where(here, line, t) if a == a0 else t
            for k in range(j + 1, group):
                m = sublanes(col[k][a0], s0) * inv
                for a in range(per):
                    t = col[k][a] - col[j][a] * m
                    col[k][a] = jnp.where(here, m, t) if a == a0 else t
        for a in range(per):
            out[first + a] = w[a]
        zb = [sublanes(z[j // 8], j % 8) for j in range(group)]
        for h in later:
            t = [mult[h][j] * zb[j] for j in range(group)]
            while len(t) > 1:
                t = [t[i] + t[i + 1] for i in range(0, len(t), 2)]
            rows[h] = rows[h] - t[0]
    return jnp.concatenate(out, axis=0)[:, 64:]


def factor_inverse_128(tile):
    t1 = factor_inverse_64(tile[:64, :64])
    u = dot(t1, tile[:64, 64:], NN)
    rest = tile[64:, 64:] - dot(u, u, TN)
    x = dot(u, t1, TN)
    t2 = factor_inverse_64(rest)
    y = -dot(t2, x, NN)
    top = jnp.concatenate([t1, jnp.zeros((64, 64), F32)], axis=1)
    return jnp.concatenate([top, jnp.concatenate([y, t2], axis=1)], axis=0)


def eye(n):
    return lax.broadcasted_iota(jnp.int32, (n, n), 0) == lax.broadcasted_iota(jnp.int32, (n, n), 1)


def kernel(
    noise_ref, cov_ref, fac_ref, tr_ref,
    s_ref, ar, ac, acc, pr, m0, m1, m2, m3,
    l_a, l_c, l_r, o_sem,
    rc, sc1, sc2, sc3, scs,
    rr, sr1, sr2, rs, ss,
    rmr, rmz, rmi, rms, sm,
):
    r = lax.axis_index("row")
    z = lax.axis_index("col")
    k = lax.rem(r, 2)
    chip = r // 2
    x = lax.rem(chip, 4)
    y = chip // 4
    u = jnp.where(k == 0, x, y)
    v = jnp.where(k == 0, y, x)

    def row_of(uu, vv):
        xx = jnp.where(k == 0, uu, vv)
        yy = jnp.where(k == 0, vv, uu)
        return (yy * 4 + xx) * 2 + k

    sib = r + 1 - 2 * k
    us = [lax.rem(u + d, 4) for d in (1, 2, 3)]
    vs = [lax.rem(v + d, 4) for d in (1, 2, 3)]
    zs = [lax.rem(z + d, 8) for d in range(1, 8)]
    u_row = [row_of(t, v) for t in us]
    v_row = [row_of(u, t) for t in vs]
    msgs = (m0, m1, m2, m3)
    head = (u == 0) & (v == 0)
    edge = v == 0
    is_root = (r == 0) & (z == 0)
    gives = (r == 1) & (z < 2)
    noise = noise_ref[0]
    pending = []

    def copy(src, dst, send, recv, row, col):
        def make():
            return pltpu.make_async_remote_copy(
                src_ref=src, dst_ref=dst, send_sem=send, recv_sem=recv, device_id=(row, col), device_id_type=MESH
            )
        return make

    def send(cond, make):
        if cond is None:
            make().start()
        else:
            @pl.when(cond)
            def _():
                make().start()
        pending.append((cond, make))

    def landed(ref, sem):
        pltpu.make_async_copy(ref, ref, sem).wait()

    def when(cond, fn):
        pl.when(cond)(fn)

    loads_a = [pltpu.make_async_copy(cov_ref.at[0, 0, :, j, 0, :], acc.at[:, pl.ds(256 * j, 256)], l_a.at[j]) for j in range(4)]
    loads_c = [pltpu.make_async_copy(cov_ref.at[0, 0, :, j, 0, :], ac.at[k, j], l_c.at[j]) for j in range(4)]
    load_r = pltpu.make_async_copy(cov_ref.at[0, 0, :, 0, 0, :], ar.at[jnp.minimum(z, 1)], l_r)

    @pl.when(z < 2)
    def _():
        load_r.start()

    @pl.when(head)
    def _():
        for q in loads_c:
            q.start()

    for q in loads_a:
        q.start()

    barrier = pltpu.get_barrier_semaphore()
    for t in u_row + v_row + [sib]:
        pl.semaphore_signal(barrier, 1, device_id=(t, z), device_id_type=MESH)
    for t in zs:
        pl.semaphore_signal(barrier, 1, device_id=(r, t), device_id_type=MESH)

    @pl.when((r == 1) & (z == 1))
    def _():
        pl.semaphore_signal(barrier, 1, device_id=(0, 0), device_id_type=MESH)

    @pl.when(is_root)
    def _():
        pl.semaphore_signal(barrier, 1, device_id=(1, 1), device_id_type=MESH)

    @pl.when(z < 2)
    def _():
        load_r.wait()

    @pl.when((r == 0) & (z != 1))
    def _():
        ar[1] = jnp.zeros((256, 256), F32)

    @pl.when(is_root)
    def _():
        s_ref[0:256, 0:256] = ar[0] + jnp.where(eye(256), noise, 0.0)
        m0[:, 0:128] = factor_inverse_128(s_ref[0:128, 0:128])

    pl.semaphore_wait(barrier, jnp.where(((r == 1) & (z == 1)) | is_root, 15, 14))

    zc = jnp.minimum(z, 1)
    send(gives, copy(ar.at[zc], s_ref.at[pl.ds(256, 256), pl.ds(256 * zc, 256)], ss, rs.at[zc], 0, 0))

    for s in range(2):
        for d in range(7):
            to = (s + d + 1) % 8
            wanted = (z == s) if s == 0 else (z == s) & (r != 0)
            part = pl.ds(32 * to, 32)
            send(wanted, copy(ar.at[s, part], ar.at[s, part], sr1.at[s, d], rr.at[s, to], r, to))

    @pl.when(head)
    def _():
        for q in loads_c:
            q.wait()

    rows = 256 // CHUNKS

    def piece(half, j, ch):
        return ac.at[half, j, pl.ds(rows * ch, rows)]

    for ch in range(CHUNKS):
        for j in (1, 2, 3):
            send(head, copy(piece(k, j, ch), piece(k, j, ch), sc1.at[j - 1, ch], rc.at[k, j, ch], row_of(j, 0), z))
    for ch in range(CHUNKS):
        mine = piece(k, u, ch)

        @pl.when(jnp.logical_not(head))
        def _():
            landed(mine, rc.at[k, u, ch])

        for d in range(3):
            send(edge, copy(mine, mine, sc2.at[d, ch], rc.at[k, u, ch], v_row[d], z))
        for d in range(3):
            wanted = jnp.logical_not((us[d] == 0) & (v == 0))
            send(wanted, copy(mine, mine, sc3.at[d, ch], rc.at[k, u, ch], u_row[d], z))
        send(None, copy(mine, mine, scs.at[0, ch], rc.at[k, u, ch], sib, z))

    for s in range(2):
        flows = None if s == 0 else r != 0
        part = pl.ds(32 * z, 32)
        wait_for = (z != s) if flows is None else (z != s) & flows

        @pl.when(wait_for)
        def _():
            landed(ar.at[s, part], rr.at[s, z])

        for d in range(7):
            wanted = (zs[d] != s) & (z != s)
            if flows is not None:
                wanted = wanted & flows
            send(wanted, copy(ar.at[s, part], ar.at[s, part], sr2.at[s, d], rr.at[s, z], r, zs[d]))
        own = (z == s) if flows is None else (z == s) & flows
        for d in range(7):
            to = (s + d + 1) % 8
            send(own, copy(ar.at[s, pl.ds(32 * s, 32)], ar.at[s, pl.ds(32 * s, 32)], sr2.at[s, d], rr.at[s, s], r, to))

    for ch in range(CHUNKS):
        for d in range(3):
            got = piece(k, us[d], ch)

            @pl.when(jnp.logical_not(head))
            def _():
                landed(got, rc.at[k, us[d], ch])

            send(None, copy(got, got, scs.at[d + 1, ch], rc.at[k, us[d], ch], sib, z))

    early = len(pending)

    def drain(which):
        for cond, make in which:
            if cond is None:
                make().wait_send()
            else:
                pl.when(cond)(lambda make=make: make().wait_send())

    def finish_inputs():
        drain(pending[:early])
        for ch in range(CHUNKS):
            for j in range(4):
                landed(piece(1 - k, j, ch), rc.at[1 - k, j, ch])
        for s in range(2):
            wanted = (z != s) if s == 0 else (z != s) & (r != 0)

            @pl.when(wanted)
            def _():
                for t in zs:
                    landed(ar.at[s, pl.ds(32 * t, 32)], rr.at[s, t])

        for q in loads_a:
            q.wait()
        for j in range(4):
            extra = jnp.where((r // 8 == j) & (lax.rem(r, 8) == z), noise, 0.0)
            sl = slice(256 * j, 256 * j + 256)
            acc[:, sl] = acc[:, sl] + jnp.where(eye(256), extra, 0.0)
        for s in range(2):
            extra = jnp.where(r == s, noise, 0.0)
            ar[s] = ar[s] + jnp.where(eye(256), extra, 0.0)

    def root_step(b):
        o = 128 * b
        if b == 0:
            landed(s_ref.at[pl.ds(256, 256), pl.ds(0, 256)], rs.at[0])
            s_ref[0:256, 256:512] = s_ref[256:512, 0:256].T
        else:
            msgs[b][:, 0:128] = factor_inverse_128(s_ref[o : o + 128, o : o + 128])
        if b == 3:
            return
        right = dot(msgs[b][:, 0:128], s_ref[o : o + 128, o + 128 :], NN)
        msgs[b][:, 128:] = right

    def root_update(b):
        if b == 0:
            landed(s_ref.at[pl.ds(256, 256), pl.ds(256, 256)], rs.at[1])
            s_ref[256:512, 256:512] = s_ref[256:512, 256:512] + jnp.where(eye(256), noise, 0.0)
        for h in range(b + 1, 4):
            left = msgs[b][:, 128 * (h - b) : 128 * (h - b) + 128]
            hl = slice(128 * h, 128 * h + 128)
            s_ref[hl, 128 * h :] = s_ref[hl, 128 * h :] - dot(left, msgs[b][:, 128 * (h - b) :], TN)

    def spread(b):
        m = msgs[b]
        half = m.at[pl.ds(64 * k, 64)]
        other = m.at[pl.ds(64 * (1 - k), 64)]
        at_source = head & (z == 0)
        send(is_root, copy(m.at[pl.ds(64, 64)], m.at[pl.ds(64, 64)], sm.at[b, 0], rmr.at[b], 1, 0))

        @pl.when((r == 1) & (z == 0))
        def _():
            landed(m.at[pl.ds(64, 64)], rmr.at[b])

        def slice_of(t):
            return m.at[pl.ds(64 * k + 8 * t, 8)]

        for t in range(1, 8):
            send(at_source, copy(slice_of(t), slice_of(t), sm.at[b, t], rmz.at[b, t], r, t))
        for t in range(1, 8):
            send(at_source, copy(slice_of(0), slice_of(0), sm.at[b, 7 + t], rmz.at[b, 0], r, t))
        relay = head & (z != 0)

        @pl.when(relay)
        def _():
            landed(slice_of(z), rmz.at[b, z])

        for d in range(7):
            send(relay & (zs[d] != 0), copy(slice_of(z), slice_of(z), sm.at[b, 15 + d], rmz.at[b, z], r, zs[d]))

        @pl.when(relay)
        def _():
            for t in zs:
                landed(slice_of(t), rmz.at[b, t])

        @pl.when(jnp.logical_not(head))
        def _():
            landed(half, rmi.at[b])

        for d in range(3):
            send(head, copy(half, half, sm.at[b, 22 + d], rmi.at[b], u_row[d], z))
        for d in range(3):
            send(edge, copy(half, half, sm.at[b, 25 + d], rmi.at[b], v_row[d], z))
        send(jnp.logical_not((r == 1) & (z == 0)), copy(half, half, sm.at[b, 28], rms.at[b], sib, z))

        @pl.when(jnp.logical_not(is_root))
        def _():
            landed(other, rms.at[b])

    grow = lax.broadcasted_iota(jnp.int32, (256, 128), 0) + 256 * r

    def panel_rows(b, last):
        m = msgs[b]
        part = slice(128 * (b % 2), 128 * (b % 2) + 128)
        p = dot(ar[b // 2, :, part], m[:, 0:128], NT)
        gcol = lax.broadcasted_iota(jnp.int32, (256, 128), 1) + 128 * b
        pr[:, 128 * b : 128 * b + 128] = jnp.where(gcol <= grow, p, 0.0)
        for h in range(b + 1, last):
            hl = slice(128 * (h % 2), 128 * (h % 2) + 128)
            ar[h // 2, :, hl] = ar[h // 2, :, hl] - dot(p, m[:, 128 * (h - b) : 128 * (h - b) + 128], NN)
        return p

    def update(b):
        m = msgs[b]
        p = panel_rows(b, 4)
        rl = slice(128 * (b % 2), 128 * (b % 2) + 128)
        for j in range(4):
            q = dot(m[:, 0:128], ac[b // 2, j, rl, :], NN)
            for h in range(b + 1, 4):
                hl = slice(128 * (h % 2), 128 * (h % 2) + 128)
                left = m[:, 128 * (h - b) : 128 * (h - b) + 128]
                ac[h // 2, j, hl, :] = ac[h // 2, j, hl, :] - dot(left, q, TN)
            sl = slice(256 * j, 256 * j + 256)
            acc[:, sl] = acc[:, sl] - dot(p, q, NN)

    for b in range(4):
        @pl.when(is_root)
        def _():
            root_step(b)

        spread(b)

        @pl.when(is_root)
        def _():
            if b < 3:
                root_update(b)

        @pl.when(jnp.logical_not(is_root))
        def _():
            if b == 0:
                finish_inputs()

        @pl.when(r != 0)
        def _():
            update(b)

    @pl.when(is_root)
    def _():
        finish_inputs()

    @pl.when(r == 0)
    def _():
        panel_rows(0, 2)
        panel_rows(1, 2)
        pr[:, 256:512] = jnp.zeros((256, 256), F32)

    for j in range(4):
        keep = (r >= 2) & (8 * j + z >= 2)
        sl = slice(256 * j, 256 * j + 256)
        acc[:, sl] = jnp.where(keep, acc[:, sl], 0.0)
    outs = [pltpu.make_async_copy(acc.at[:, pl.ds(256 * j, 256)], tr_ref.at[0, 0, :, j, 0, :], o_sem.at[j]) for j in range(4)]
    outs += [pltpu.make_async_copy(pr.at[:, pl.ds(256 * j, 256)], fac_ref.at[0, 0, :, j, :], o_sem.at[4 + j]) for j in range(2)]
    for q in outs:
        q.start()
    drain(pending[early:])
    for q in outs:
        q.wait()


def body(cov, noise):
    anywhere = pl.BlockSpec(memory_space=pl.ANY)
    dma = pltpu.SemaphoreType.DMA
    return pl.pallas_call(
        kernel,
        in_specs=[pl.BlockSpec(memory_space=pltpu.SMEM), anywhere],
        out_specs=[anywhere, anywhere],
        out_shape=[
            jax.ShapeDtypeStruct((1, 1, 256, 2, 256), F32),
            jax.ShapeDtypeStruct((1, 1, 256, 4, 1, 256), F32),
        ],
        scratch_shapes=[
            pltpu.VMEM((512, 512), F32),
            pltpu.VMEM((2, 256, 256), F32),
            pltpu.VMEM((2, 4, 256, 256), F32),
            pltpu.VMEM((256, 1024), F32),
            pltpu.VMEM((256, 512), F32),
        ]
        + [pltpu.VMEM((128, w), F32) for w in WIDTHS]
        + [
            dma((4,)), dma((4,)), dma, dma((6,)),
            dma((2, 4, CHUNKS)), dma((3, CHUNKS)), dma((3, CHUNKS)), dma((3, CHUNKS)), dma((4, CHUNKS)),
            dma((2, 8)), dma((2, 7)), dma((2, 7)), dma((2,)), dma,
            dma((4,)), dma((4, 8)), dma((4,)), dma((4,)), dma((4, 29)),
        ],
        compiler_params=pltpu.CompilerParams(collective_id=0, has_side_effects=True, vmem_limit_bytes=40 * 2**20),
    )(noise.reshape(1), cov)


def solution(mesh):
    return jax.shard_map(
        body,
        mesh=mesh,
        in_specs=(P(None, "row", None, None, "col", None), P()),
        out_specs=(P(None, "row", None, None, None), P(None, "row", None, None, "col", None)),
        check_vma=False,
    )
```

```python
import jax
import jax.numpy as jnp
from jax import lax
from jax.experimental import pallas as pl
from jax.experimental.pallas import tpu as pltpu
from jax.sharding import PartitionSpec as P

F32 = jnp.float32
NN = ((1,), (0,))
TN = ((0,), (0,))
NT = ((1,), (1,))
MESH = pl.DeviceIdType.MESH
CHUNKS = 4
WIDTHS = (512, 384, 256, 128)
FAR_FIRST = (10, 9, 11, 6, 14, 2, 8, 5, 7, 13, 15, 1, 3, 4, 12)


def split(a):
    hi = a.astype(jnp.bfloat16)
    return hi, (a - hi.astype(F32)).astype(jnp.bfloat16)


def dot(a, b, dims):
    a = a if isinstance(a, tuple) else split(a)
    b = b if isinstance(b, tuple) else split(b)

    def one(i, j):
        return lax.dot_general(a[i], b[j], (dims, ((), ())), preferred_element_type=F32)

    return one(0, 0) + (one(0, 1) + one(1, 0))


def lanes(v, q):
    return jnp.broadcast_to(v[:, q : q + 1], (8, 128))


def sublanes(v, j):
    return jnp.broadcast_to(v[j : j + 1, :], (8, 128))


def factor_inverse_64(tile, group=16):
    count = 8
    per = group // 8
    sub = lax.broadcasted_iota(jnp.int32, (8, 128), 0)
    lane = lax.broadcasted_iota(jnp.int32, (8, 128), 1)
    rows = []
    for h in range(count):
        left = jnp.concatenate([tile[8 * h : 8 * h + 8, :], jnp.zeros((8, 64), F32)], axis=1)
        rows.append(jnp.where(lane < 64, left, (lane - 64 == sub + 8 * h).astype(F32)))
    out = [None] * count
    for g in range(64 // group):
        first = g * per
        col = [[lanes(rows[first + a], group * g + j) for a in range(per)] for j in range(group)]
        later = range(first + per, count)
        mult = {h: [lanes(rows[h], group * g + j) for j in range(group)] for h in later}
        z = [rows[first + a] for a in range(per)]
        w = [jnp.zeros((8, 128), F32) for _ in range(per)]
        pivot = sublanes(col[0][0], 0)
        for j in range(group):
            a0, s0 = j // 8, j % 8
            here = sub == s0
            inv = 1.0 / pivot
            root = lax.rsqrt(pivot)
            if j + 1 < group:
                a1, s1 = (j + 1) // 8, (j + 1) % 8
                cross = sublanes(col[j][a1], s1) * sublanes(col[j + 1][a0], s0)
                pivot = sublanes(col[j + 1][a1], s1) - cross * inv
            line = sublanes(z[a0], s0)
            w[a0] = jnp.where(here, line * root, w[a0])
            line = line * inv
            for a in range(per):
                t = z[a] - col[j][a] * line
                z[a] = jnp.where(here, line, t) if a == a0 else t
            for k in range(j + 1, group):
                m = sublanes(col[k][a0], s0) * inv
                for a in range(per):
                    t = col[k][a] - col[j][a] * m
                    col[k][a] = jnp.where(here, m, t) if a == a0 else t
        for a in range(per):
            out[first + a] = w[a]
        zb = [sublanes(z[j // 8], j % 8) for j in range(group)]
        for h in later:
            t = [mult[h][j] * zb[j] for j in range(group)]
            while len(t) > 1:
                t = [t[i] + t[i + 1] for i in range(0, len(t), 2)]
            rows[h] = rows[h] - t[0]
    return jnp.concatenate(out, axis=0)[:, 64:]


def factor_inverse_128(tile):
    t1 = factor_inverse_64(tile[:64, :64])
    t1s = split(t1)
    u = split(dot(t1s, tile[:64, 64:], NN))
    rest = tile[64:, 64:] - dot(u, u, TN)
    x = dot(u, t1s, TN)
    t2 = factor_inverse_64(rest)
    y = -dot(t2, x, NN)
    top = jnp.concatenate([t1, jnp.zeros((64, 64), F32)], axis=1)
    return jnp.concatenate([top, jnp.concatenate([y, t2], axis=1)], axis=0)


def eye(n):
    return lax.broadcasted_iota(jnp.int32, (n, n), 0) == lax.broadcasted_iota(jnp.int32, (n, n), 1)


def kernel(
    noise_hbm, cov_ref, fac_ref, tr_ref,
    noise_ref, l_n, s_ref, ar, ac, acc, pr, m0, m1, m2, m3,
    l_a, l_c, l_r, o_sem,
    rc, sc1, sc2, sc3, scs,
    rr, sr1, sr2, rs, ss,
    rmr, rmq, rms, sm,
):
    r = lax.axis_index("row")
    z = lax.axis_index("col")
    k = lax.rem(r, 2)
    chip = r // 2
    x = lax.rem(chip, 4)
    y = chip // 4
    u = jnp.where(k == 0, x, y)
    v = jnp.where(k == 0, y, x)

    def row_of(uu, vv):
        xx = jnp.where(k == 0, uu, vv)
        yy = jnp.where(k == 0, vv, uu)
        return (yy * 4 + xx) * 2 + k

    sib = r + 1 - 2 * k
    us = [lax.rem(u + d, 4) for d in (1, 2, 3)]
    vs = [lax.rem(v + d, 4) for d in (1, 2, 3)]
    zs = [lax.rem(z + d, 8) for d in range(1, 8)]
    u_row = [row_of(t, v) for t in us]
    v_row = [row_of(u, t) for t in vs]
    chips = [lax.rem(chip + d, 16) for d in range(1, 16)]
    plane = [2 * t + k for t in chips]
    msgs = (m0, m1, m2, m3)
    head = (u == 0) & (v == 0)
    edge = v == 0
    is_root = (r == 0) & (z == 0)
    helper = (r == 1) & (z == 0)
    gives = (r == 1) & (z < 2)
    pending = []

    def copy(src, dst, send, recv, row, col):
        def make():
            return pltpu.make_async_remote_copy(
                src_ref=src, dst_ref=dst, send_sem=send, recv_sem=recv, device_id=(row, col), device_id_type=MESH
            )
        return make

    def send(cond, make):
        if cond is None:
            make().start()
        else:
            @pl.when(cond)
            def _():
                make().start()
        pending.append((cond, make))

    def landed(ref, sem):
        pltpu.make_async_copy(ref, ref, sem).wait()

    def when(cond, fn):
        pl.when(cond)(fn)

    loads_a = [pltpu.make_async_copy(cov_ref.at[0, 0, :, j, 0, :], acc.at[:, pl.ds(256 * j, 256)], l_a.at[j]) for j in range(4)]
    loads_c = [pltpu.make_async_copy(cov_ref.at[0, 0, :, j, 0, :], ac.at[k, j], l_c.at[j]) for j in range(4)]
    load_r = pltpu.make_async_copy(cov_ref.at[0, 0, :, 0, 0, :], ar.at[jnp.minimum(z, 1)], l_r)

    @pl.when(z < 2)
    def _():
        load_r.start()

    @pl.when(head)
    def _():
        for q in loads_c:
            q.start()

    for q in loads_a:
        q.start()
    load_n = pltpu.make_async_copy(noise_hbm, noise_ref, l_n)
    load_n.start()

    barrier = pltpu.get_barrier_semaphore()
    for t in plane + [sib]:
        pl.semaphore_signal(barrier, 1, device_id=(t, z), device_id_type=MESH)
    for t in zs:
        pl.semaphore_signal(barrier, 1, device_id=(r, t), device_id_type=MESH)

    @pl.when((r == 1) & (z == 1))
    def _():
        pl.semaphore_signal(barrier, 1, device_id=(0, 0), device_id_type=MESH)

    @pl.when(is_root)
    def _():
        pl.semaphore_signal(barrier, 1, device_id=(1, 1), device_id_type=MESH)

    load_n.wait()
    noise = noise_ref[0]

    @pl.when(z < 2)
    def _():
        load_r.wait()

    @pl.when((r == 0) & (z != 1))
    def _():
        ar[1] = jnp.zeros((256, 256), F32)

    @pl.when(is_root)
    def _():
        s_ref[0:256, 0:256] = ar[0] + jnp.where(eye(256), noise, 0.0)
        m0[:, 0:128] = factor_inverse_128(s_ref[0:128, 0:128])

    pl.semaphore_wait(barrier, 23 + jnp.where(((r == 1) & (z == 1)) | is_root, 1, 0))

    zc = jnp.minimum(z, 1)
    send(gives, copy(ar.at[zc], s_ref.at[pl.ds(256, 256), pl.ds(256 * zc, 256)], ss, rs.at[zc], 0, 0))

    for s in range(2):
        for d in range(7):
            to = (s + d + 1) % 8
            wanted = (z == s) if s == 0 else (z == s) & (r != 0)
            part = pl.ds(32 * to, 32)
            send(wanted, copy(ar.at[s, part], ar.at[s, part], sr1.at[s, d], rr.at[s, to], r, to))

    @pl.when(head)
    def _():
        for q in loads_c:
            q.wait()

    rows = 256 // CHUNKS

    def piece(half, j, ch):
        return ac.at[half, j, pl.ds(rows * ch, rows)]

    for ch in range(CHUNKS):
        for j in (1, 2, 3):
            send(head, copy(piece(k, j, ch), piece(k, j, ch), sc1.at[j - 1, ch], rc.at[k, j, ch], row_of(j, 0), z))
    for ch in range(CHUNKS):
        mine = piece(k, u, ch)

        @pl.when(jnp.logical_not(head))
        def _():
            landed(mine, rc.at[k, u, ch])

        for d in range(3):
            send(edge, copy(mine, mine, sc2.at[d, ch], rc.at[k, u, ch], v_row[d], z))
        for d in range(3):
            wanted = jnp.logical_not((us[d] == 0) & (v == 0))
            send(wanted, copy(mine, mine, sc3.at[d, ch], rc.at[k, u, ch], u_row[d], z))
        send(None, copy(mine, mine, scs.at[0, ch], rc.at[k, u, ch], sib, z))

    for s in range(2):
        flows = None if s == 0 else r != 0
        part = pl.ds(32 * z, 32)
        wait_for = (z != s) if flows is None else (z != s) & flows

        @pl.when(wait_for)
        def _():
            landed(ar.at[s, part], rr.at[s, z])

        for d in range(7):
            wanted = (zs[d] != s) & (z != s)
            if flows is not None:
                wanted = wanted & flows
            send(wanted, copy(ar.at[s, part], ar.at[s, part], sr2.at[s, d], rr.at[s, z], r, zs[d]))
        own = (z == s) if flows is None else (z == s) & flows
        for d in range(7):
            to = (s + d + 1) % 8
            send(own, copy(ar.at[s, pl.ds(32 * s, 32)], ar.at[s, pl.ds(32 * s, 32)], sr2.at[s, d], rr.at[s, s], r, to))

    def pass_on():
        for ch in range(CHUNKS):
            for d in range(3):
                got = piece(k, us[d], ch)

                @pl.when(jnp.logical_not(head))
                def _():
                    landed(got, rc.at[k, us[d], ch])

                send(None, copy(got, got, scs.at[d + 1, ch], rc.at[k, us[d], ch], sib, z))

    def drain(which):
        for cond, make in which:
            if cond is None:
                make().wait_send()
            else:
                pl.when(cond)(lambda make=make: make().wait_send())

    def finish_inputs():
        drain(inputs_sent)
        for ch in range(CHUNKS):
            for j in range(4):
                landed(piece(1 - k, j, ch), rc.at[1 - k, j, ch])
        for s in range(2):
            wanted = (z != s) if s == 0 else (z != s) & (r != 0)

            @pl.when(wanted)
            def _():
                for t in zs:
                    landed(ar.at[s, pl.ds(32 * t, 32)], rr.at[s, t])

        for q in loads_a:
            q.wait()
        for j in range(4):
            extra = jnp.where((r // 8 == j) & (lax.rem(r, 8) == z), noise, 0.0)
            sl = slice(256 * j, 256 * j + 256)
            acc[:, sl] = acc[:, sl] + jnp.where(eye(256), extra, 0.0)
        for s in range(2):
            extra = jnp.where(r == s, noise, 0.0)
            ar[s] = ar[s] + jnp.where(eye(256), extra, 0.0)

    def left_of(b, h):
        return msgs[b][:, 128 * (h - b) : 128 * (h - b) + 128]

    def root_step(b):
        o = 128 * b
        if b == 0:
            landed(s_ref.at[pl.ds(256, 256), pl.ds(0, 256)], rs.at[0])
            s_ref[0:256, 256:512] = s_ref[256:512, 0:256].T
        else:
            c = b - 1
            if c == 0:
                landed(s_ref.at[pl.ds(256, 256), pl.ds(256, 256)], rs.at[1])
                s_ref[256:512, 256:512] = s_ref[256:512, 256:512] + jnp.where(eye(256), noise, 0.0)
            lefts = {h: split(left_of(c, h)) for h in range(b, 4)}
            tile = s_ref[o : o + 128, o : o + 128] - dot(lefts[b], lefts[b], TN)
            msgs[b][:, 0:128] = factor_inverse_128(tile)
            for h in range(b, 4):
                hl = slice(128 * h, 128 * h + 128)
                for w in range(max(h, b + 1), 4):
                    wl = slice(128 * w, 128 * w + 128)
                    s_ref[hl, wl] = s_ref[hl, wl] - dot(lefts[h], lefts[w], TN)
        if b < 3:
            msgs[b][:, 128:] = dot(msgs[b][:, 0:128], s_ref[o : o + 128, o + 128 :], NN)

    inputs_sent = list(pending)

    def share(b, q):
        return msgs[b].at[pl.ds(pl.multiple_of(8 * q, 8), 8)]

    def carrier(b):
        return 0 if b == 3 else 1

    def relay(b):
        m = msgs[b]
        kb = carrier(b)
        source = (r == kb) & (z == 0)
        carries = k == kb
        if b < 3:
            send(is_root, copy(m, m, sm.at[b, 0], rmr.at[b], 1, 0))

            @pl.when(helper)
            def _():
                landed(m, rmr.at[b])

        for n, q in enumerate(FAR_FIRST):
            send(source, copy(share(b, q), share(b, q), sm.at[b, 1 + n], rmq.at[b, q], 2 * q + kb, 0))
        mine = share(b, chip)

        @pl.when(carries & jnp.logical_not(source))
        def _():
            landed(mine, rmq.at[b, chip])

        for d in range(7):
            send(carries & (z == 0), copy(mine, mine, sm.at[b, 16 + d], rmq.at[b, chip], r, zs[d]))
        for d in range(15):
            wanted = carries & jnp.logical_not((chips[d] == 0) & (z == 0))
            send(wanted, copy(mine, mine, sm.at[b, 23 + d], rmq.at[b, chip], plane[d], z))
        if b == 3:
            send(source, copy(m, m, sm.at[b, 38], rms.at[b], sib, z))

    def collect(b):
        m = msgs[b]
        kb = carrier(b)
        source = (r == kb) & (z == 0)
        carries = (k == kb) & jnp.logical_not(source)

        @pl.when(carries)
        def _():
            for t in chips:
                landed(share(b, t), rmq.at[b, t])

        send(carries, copy(m, m, sm.at[b, 38], rms.at[b], sib, z))
        has = (k == kb) | is_root if b < 3 else k == kb

        @pl.when(jnp.logical_not(has))
        def _():
            landed(m, rms.at[b])

    grow = lax.broadcasted_iota(jnp.int32, (256, 128), 0) + 256 * r

    def panel_rows(b, last):
        m = msgs[b]
        part = slice(128 * (b % 2), 128 * (b % 2) + 128)
        ts = split(m[:, 0:128])
        p = dot(ar[b // 2, :, part], ts, NT)
        gcol = lax.broadcasted_iota(jnp.int32, (256, 128), 1) + 128 * b
        pr[:, 128 * b : 128 * b + 128] = jnp.where(gcol <= grow, p, 0.0)
        ps = split(p)
        lefts = {h: split(left_of(b, h)) for h in range(b + 1, last)}
        for h in range(b + 1, last):
            hl = slice(128 * (h % 2), 128 * (h % 2) + 128)
            ar[h // 2, :, hl] = ar[h // 2, :, hl] - dot(ps, lefts[h], NN)
        return ts, ps, lefts

    def update(b):
        ts, ps, lefts = panel_rows(b, 4)
        rl = slice(128 * (b % 2), 128 * (b % 2) + 128)
        for j in range(4):
            q = split(dot(ts, ac[b // 2, j, rl, :], NN))
            for h in range(b + 1, 4):
                hl = slice(128 * (h % 2), 128 * (h % 2) + 128)
                ac[h // 2, j, hl, :] = ac[h // 2, j, hl, :] - dot(lefts[h], q, TN)
            sl = slice(256 * j, 256 * j + 256)
            acc[:, sl] = acc[:, sl] - dot(ps, q, NN)

    def step(b):
        @pl.when(r >= 2)
        def _():
            update(b)

    for b in range(4):
        @pl.when(is_root)
        def _():
            root_step(b)

        if b < 3:
            relay(b)
    relay(3)
    before = len(pending)
    pass_on()
    inputs_sent += pending[before:]
    collect(0)
    collect(1)
    collect(2)
    finish_inputs()
    step(0)
    step(1)
    step(2)
    collect(3)
    step(3)

    @pl.when(r == 0)
    def _():
        panel_rows(0, 2)
        panel_rows(1, 2)
        pr[:, 256:512] = jnp.zeros((256, 256), F32)

    @pl.when(r == 1)
    def _():
        for b in range(4):
            panel_rows(b, 4)

    for j in range(4):
        keep = (r >= 2) & (8 * j + z >= 2)
        sl = slice(256 * j, 256 * j + 256)
        acc[:, sl] = jnp.where(keep, acc[:, sl], 0.0)
    outs = [pltpu.make_async_copy(acc.at[:, pl.ds(256 * j, 256)], tr_ref.at[0, 0, :, j, 0, :], o_sem.at[j]) for j in range(4)]
    outs += [pltpu.make_async_copy(pr.at[:, pl.ds(256 * j, 256)], fac_ref.at[0, 0, :, j, :], o_sem.at[4 + j]) for j in range(2)]
    for q in outs:
        q.start()
    done = {id(e) for e in inputs_sent}
    drain([e for e in pending if id(e) not in done])
    for q in outs:
        q.wait()


def body(cov, noise):
    anywhere = pl.BlockSpec(memory_space=pl.ANY)
    dma = pltpu.SemaphoreType.DMA
    return pl.pallas_call(
        kernel,
        in_specs=[anywhere, anywhere],
        out_specs=[anywhere, anywhere],
        out_shape=[
            jax.ShapeDtypeStruct((1, 1, 256, 2, 256), F32),
            jax.ShapeDtypeStruct((1, 1, 256, 4, 1, 256), F32),
        ],
        scratch_shapes=[
            pltpu.SMEM((1,), F32),
            dma,
            pltpu.VMEM((512, 512), F32),
            pltpu.VMEM((2, 256, 256), F32),
            pltpu.VMEM((2, 4, 256, 256), F32),
            pltpu.VMEM((256, 1024), F32),
            pltpu.VMEM((256, 512), F32),
        ]
        + [pltpu.VMEM((128, w), F32) for w in WIDTHS]
        + [
            dma((4,)), dma((4,)), dma, dma((6,)),
            dma((2, 4, CHUNKS)), dma((3, CHUNKS)), dma((3, CHUNKS)), dma((3, CHUNKS)), dma((4, CHUNKS)),
            dma((2, 8)), dma((2, 7)), dma((2, 7)), dma((2,)), dma,
            dma((4,)), dma((4, 16)), dma((4,)), dma((4, 39)),
        ],
        compiler_params=pltpu.CompilerParams(collective_id=0, has_side_effects=True, vmem_limit_bytes=40 * 2**20),
    )(noise.reshape(1), cov)


def solution(mesh):
    return jax.shard_map(
        body,
        mesh=mesh,
        in_specs=(P(None, "row", None, None, "col", None), P()),
        out_specs=(P(None, "row", None, None, None), P(None, "row", None, None, "col", None)),
        check_vma=False,
    )
```

```python
import jax
import jax.numpy as jnp
from jax import lax
from jax.experimental import pallas as pl
from jax.experimental.pallas import tpu as pltpu
from jax.sharding import PartitionSpec as P

F32 = jnp.float32
NN = ((1,), (0,))
TN = ((0,), (0,))
NT = ((1,), (1,))
MESH = pl.DeviceIdType.MESH
CHUNKS = 4
WIDTHS = (512, 384, 256, 128)
FAR_FIRST = (10, 9, 11, 6, 14, 2, 8, 5, 7, 13, 15, 1, 3, 4, 12)


def split(a):
    hi = a.astype(jnp.bfloat16)
    return hi, (a - hi.astype(F32)).astype(jnp.bfloat16)


def dot(a, b, dims):
    a = a if isinstance(a, tuple) else split(a)
    b = b if isinstance(b, tuple) else split(b)

    def one(i, j):
        return lax.dot_general(a[i], b[j], (dims, ((), ())), preferred_element_type=F32)

    return one(0, 0) + (one(0, 1) + one(1, 0))


def lanes(v, q):
    return jnp.broadcast_to(v[:, q : q + 1], (8, 128))


def sublanes(v, j):
    return jnp.broadcast_to(v[j : j + 1, :], (8, 128))


def factor_inverse_64(tile, group=16):
    count = 8
    per = group // 8
    sub = lax.broadcasted_iota(jnp.int32, (8, 128), 0)
    lane = lax.broadcasted_iota(jnp.int32, (8, 128), 1)
    rows = []
    for h in range(count):
        left = jnp.concatenate([tile[8 * h : 8 * h + 8, :], jnp.zeros((8, 64), F32)], axis=1)
        rows.append(jnp.where(lane < 64, left, (lane - 64 == sub + 8 * h).astype(F32)))
    out = [None] * count
    for g in range(64 // group):
        first = g * per
        col = [[lanes(rows[first + a], group * g + j) for a in range(per)] for j in range(group)]
        later = range(first + per, count)
        mult = {h: [lanes(rows[h], group * g + j) for j in range(group)] for h in later}
        z = [rows[first + a] for a in range(per)]
        w = [jnp.zeros((8, 128), F32) for _ in range(per)]
        pivot = sublanes(col[0][0], 0)
        for j in range(group):
            a0, s0 = j // 8, j % 8
            here = sub == s0
            inv = 1.0 / pivot
            root = lax.rsqrt(pivot)
            if j + 1 < group:
                a1, s1 = (j + 1) // 8, (j + 1) % 8
                cross = sublanes(col[j][a1], s1) * sublanes(col[j + 1][a0], s0)
                pivot = sublanes(col[j + 1][a1], s1) - cross * inv
            line = sublanes(z[a0], s0)
            w[a0] = jnp.where(here, line * root, w[a0])
            line = line * inv
            for a in range(per):
                t = z[a] - col[j][a] * line
                z[a] = jnp.where(here, line, t) if a == a0 else t
            for k in range(j + 1, group):
                m = sublanes(col[k][a0], s0) * inv
                for a in range(per):
                    t = col[k][a] - col[j][a] * m
                    col[k][a] = jnp.where(here, m, t) if a == a0 else t
        for a in range(per):
            out[first + a] = w[a]
        zb = [sublanes(z[j // 8], j % 8) for j in range(group)]
        for h in later:
            t = [mult[h][j] * zb[j] for j in range(group)]
            while len(t) > 1:
                t = [t[i] + t[i + 1] for i in range(0, len(t), 2)]
            rows[h] = rows[h] - t[0]
    return jnp.concatenate(out, axis=0)[:, 64:]


def factor_inverse_128(tile, t1=None):
    if t1 is None:
        t1 = factor_inverse_64(tile[:64, :64])
    t1s = split(t1)
    u = split(dot(t1s, tile[:64, 64:], NN))
    rest = tile[64:, 64:] - dot(u, u, TN)
    x = dot(u, t1s, TN)
    t2 = factor_inverse_64(rest)
    y = -dot(t2, x, NN)
    top = jnp.concatenate([t1, jnp.zeros((64, 64), F32)], axis=1)
    return jnp.concatenate([top, jnp.concatenate([y, t2], axis=1)], axis=0)


def eye(n):
    return lax.broadcasted_iota(jnp.int32, (n, n), 0) == lax.broadcasted_iota(jnp.int32, (n, n), 1)


def kernel(
    noise_hbm, cov_ref, fac_ref, tr_ref,
    noise_ref, l_n, s_ref, ar, ac, acc, pr, m0, m1, m2, m3,
    l_a, l_c, l_r, o_sem,
    rc, sc1, sc2, sc3, scs,
    rr, ro, sr1, sr2, rs, ss,
    rmr, rmo, rmq, rms, sm,
):
    r = lax.axis_index("row")
    z = lax.axis_index("col")
    k = lax.rem(r, 2)
    chip = r // 2
    x = lax.rem(chip, 4)
    y = chip // 4
    u = jnp.where(k == 0, x, y)
    v = jnp.where(k == 0, y, x)

    def row_of(uu, vv):
        xx = jnp.where(k == 0, uu, vv)
        yy = jnp.where(k == 0, vv, uu)
        return (yy * 4 + xx) * 2 + k

    sib = r + 1 - 2 * k
    us = [lax.rem(u + d, 4) for d in (1, 2, 3)]
    vs = [lax.rem(v + d, 4) for d in (1, 2, 3)]
    zs = [lax.rem(z + d, 8) for d in range(1, 8)]
    u_row = [row_of(t, v) for t in us]
    v_row = [row_of(u, t) for t in vs]
    chips = [lax.rem(chip + d, 16) for d in range(1, 16)]
    plane = [2 * t + k for t in chips]
    msgs = (m0, m1, m2, m3)
    head = (u == 0) & (v == 0)
    is_root = (r == 0) & (z == 0)
    helper = (r == 1) & (z == 0)
    gives = (r == 1) & (z < 2)
    pending = []

    def copy(src, dst, send, recv, row, col):
        def make():
            return pltpu.make_async_remote_copy(
                src_ref=src, dst_ref=dst, send_sem=send, recv_sem=recv, device_id=(row, col), device_id_type=MESH
            )
        return make

    def start(cond, *makes):
        if cond is None:
            for make in makes:
                make().start()
        else:
            @pl.when(cond)
            def _():
                for make in makes:
                    make().start()

    def owe(cond, ref, sem):
        pending.append((cond, ref, sem))

    def landed(ref, sem):
        pltpu.make_async_copy(ref, ref, sem).wait()

    def when(cond, fn):
        pl.when(cond)(fn)

    loads_a = [pltpu.make_async_copy(cov_ref.at[0, 0, :, j, 0, :], acc.at[:, pl.ds(256 * j, 256)], l_a.at[j]) for j in range(4)]
    loads_c = [pltpu.make_async_copy(cov_ref.at[0, 0, :, j, 0, :], ac.at[k, j], l_c.at[j]) for j in range(4)]
    load_r = pltpu.make_async_copy(cov_ref.at[0, 0, :, 0, 0, :], ar.at[jnp.minimum(z, 1)], l_r)

    @pl.when(z < 2)
    def _():
        load_r.start()

    @pl.when(head)
    def _():
        for q in loads_c:
            q.start()

    for q in loads_a:
        q.start()
    load_n = pltpu.make_async_copy(noise_hbm, noise_ref, l_n)
    load_n.start()

    barrier = pltpu.get_barrier_semaphore()
    for t in plane + [sib]:
        pl.semaphore_signal(barrier, 1, device_id=(t, z), device_id_type=MESH)
    for t in zs:
        pl.semaphore_signal(barrier, 1, device_id=(r, t), device_id_type=MESH)

    @pl.when((r == 1) & (z == 1))
    def _():
        pl.semaphore_signal(barrier, 1, device_id=(0, 0), device_id_type=MESH)

    @pl.when(is_root)
    def _():
        pl.semaphore_signal(barrier, 1, device_id=(1, 1), device_id_type=MESH)

    load_n.wait()
    noise = noise_ref[0]

    @pl.when(z < 2)
    def _():
        load_r.wait()

    @pl.when((r == 0) & (z != 1))
    def _():
        ar[1] = jnp.zeros((256, 256), F32)

    @pl.when(is_root)
    def _():
        s_ref[0:256, 0:256] = ar[0] + jnp.where(eye(256), noise, 0.0)
        m0[0:64, 0:64] = factor_inverse_64(s_ref[0:64, 0:64])

    pl.semaphore_wait(barrier, 23 + jnp.where(((r == 1) & (z == 1)) | is_root, 1, 0))

    zc = jnp.minimum(z, 1)
    start(gives, copy(ar.at[zc], s_ref.at[pl.ds(256, 256), pl.ds(256 * zc, 256)], ss, rs.at[zc], 0, 0))
    owe(gives, ar.at[zc], ss)

    owners = (z == 0, (z == 1) & (r != 0))
    relays = (z != 0, (z != 1) & (r != 0))
    for s in range(2):
        makes = []
        for d in range(7):
            to = (s + d + 1) % 8
            part = ar.at[s, pl.ds(32 * to, 32)]
            makes.append(copy(part, part, sr1.at[s], ro.at[s], r, to))
        start(owners[s], *makes)
        owe(owners[s], ar.at[s, pl.ds(0, 224)], sr1.at[s])

    @pl.when(head)
    def _():
        for q in loads_c:
            q.wait()

    rows = 256 // CHUNKS

    def piece(half, j, ch):
        return ac.at[half, j, pl.ds(rows * ch, rows)]

    off_head = jnp.logical_not(head)
    for ch in range(CHUNKS):
        makes = [copy(piece(k, j, ch), piece(k, j, ch), sc1, rc.at[k, j, ch], row_of(j, 0), z) for j in (2, 1, 3)]
        start(head, *makes, copy(piece(k, 0, ch), piece(k, 0, ch), sc1, rc.at[k, 0, ch], row_of(0, 2), z))
    owe(head, ac.at[k], sc1)
    deals = (v == 0) & (u != 0)
    again = (v == 2) & (u == 0)
    skips = (v == 0) & (u != 0)
    for ch in range(CHUNKS):
        mine = piece(k, u, ch)

        @pl.when(off_head)
        def _():
            landed(mine, rc.at[k, u, ch])

        start(deals, *[copy(mine, mine, sc2, rc.at[k, u, ch], v_row[d], z) for d in (1, 0, 2)])
        start(again, *[copy(mine, mine, sc2, rc.at[k, u, ch], row_of(0, t), z) for t in (1, 3)])
        for d in (1, 0, 2):
            start((v != 0) | (us[d] != 0), copy(mine, mine, sc3, rc.at[k, u, ch], u_row[d], z))
        start(None, copy(mine, mine, scs, rc.at[k, u, ch], sib, z))
    owe(deals, ac.at[k, pl.ds(0, 3)], sc2)
    owe(again, ac.at[k, pl.ds(0, 2)], sc2)
    owe(skips, ac.at[k, pl.ds(0, 2)], sc3)
    owe(jnp.logical_not(skips), ac.at[k, pl.ds(0, 3)], sc3)

    for s in range(2):
        part = ar.at[s, pl.ds(32 * z, 32)]

        @pl.when(relays[s])
        def _():
            landed(part, ro.at[s])
            for d in range(7):
                start(zs[d] != s, copy(part, part, sr2.at[s], rr.at[s], r, zs[d]))

        owe(relays[s], ar.at[s, pl.ds(0, 192)], sr2.at[s])
        first = ar.at[s, pl.ds(32 * s, 32)]
        start(owners[s], *[copy(first, first, sr2.at[s], rr.at[s], r, (s + d + 1) % 8) for d in range(7)])
        owe(owners[s], ar.at[s, pl.ds(0, 224)], sr2.at[s])

    def pass_on():
        for ch in range(CHUNKS):
            for d in range(3):
                got = piece(k, us[d], ch)

                @pl.when(jnp.logical_not(head))
                def _():
                    landed(got, rc.at[k, us[d], ch])

                start(None, copy(got, got, scs, rc.at[k, us[d], ch], sib, z))
        owe(None, ac.at[k], scs)

    def drain(which):
        for cond, ref, sem in which:
            if cond is None:
                landed(ref, sem)
            else:
                pl.when(cond)(lambda ref=ref, sem=sem: landed(ref, sem))

    def finish_inputs():
        drain(inputs_sent)
        for ch in range(CHUNKS):
            for j in range(4):
                landed(piece(1 - k, j, ch), rc.at[1 - k, j, ch])
        for s in range(2):
            @pl.when(relays[s])
            def _():
                landed(ar.at[s, pl.ds(0, 224)], rr.at[s])

        for q in loads_a:
            q.wait()
        for j in range(4):
            extra = jnp.where((r // 8 == j) & (lax.rem(r, 8) == z), noise, 0.0)
            sl = slice(256 * j, 256 * j + 256)
            acc[:, sl] = acc[:, sl] + jnp.where(eye(256), extra, 0.0)
        for s in range(2):
            extra = jnp.where(r == s, noise, 0.0)
            ar[s] = ar[s] + jnp.where(eye(256), extra, 0.0)

    def left_of(b, h):
        return msgs[b][:, 128 * (h - b) : 128 * (h - b) + 128]

    def root_step(b):
        o = 128 * b
        if b == 0:
            m0[:, 0:128] = factor_inverse_128(s_ref[0:128, 0:128], m0[0:64, 0:64])
            landed(s_ref.at[pl.ds(256, 256), pl.ds(0, 256)], rs.at[0])
            s_ref[0:256, 256:512] = s_ref[256:512, 0:256].T
        else:
            c = b - 1
            if c == 0:
                landed(s_ref.at[pl.ds(256, 256), pl.ds(256, 256)], rs.at[1])
                s_ref[256:512, 256:512] = s_ref[256:512, 256:512] + jnp.where(eye(256), noise, 0.0)
            lefts = {h: split(left_of(c, h)) for h in range(b, 4)}
            tile = s_ref[o : o + 128, o : o + 128] - dot(lefts[b], lefts[b], TN)
            msgs[b][:, 0:128] = factor_inverse_128(tile)
            for h in range(b, 4):
                hl = slice(128 * h, 128 * h + 128)
                for w in range(max(h, b + 1), 4):
                    wl = slice(128 * w, 128 * w + 128)
                    s_ref[hl, wl] = s_ref[hl, wl] - dot(lefts[h], lefts[w], TN)
        if b < 3:
            msgs[b][:, 128:] = dot(msgs[b][:, 0:128], s_ref[o : o + 128, o + 128 :], NN)

    inputs_sent = list(pending)

    def share(b, q):
        return msgs[b].at[pl.ds(pl.multiple_of(8 * q, 8), 8)]

    def carrier(b):
        return 0 if b == 3 else 1

    def relay(b):
        m = msgs[b]
        kb = carrier(b)
        source = (r == kb) & (z == 0)
        carries = k == kb
        if b < 3:
            start(is_root, copy(m, m, sm.at[b, 0], rmr.at[b], 1, 0))
            owe(is_root, m, sm.at[b, 0])

            @pl.when(helper)
            def _():
                landed(m, rmr.at[b])

        start(source, *[copy(share(b, q), share(b, q), sm.at[b, 1], rmo.at[b], 2 * q + kb, 0) for q in FAR_FIRST])
        owe(source, m.at[pl.ds(0, 120)], sm.at[b, 1])
        mine = share(b, chip)

        @pl.when(carries & jnp.logical_not(source))
        def _():
            landed(mine, rmo.at[b])

        deal_z = carries & (z == 0)
        start(deal_z, *[copy(mine, mine, sm.at[b, 2], rmo.at[b], r, zs[d]) for d in range(7)])
        owe(deal_z, m.at[pl.ds(0, 56)], sm.at[b, 2])
        full = carries & ((z != 0) | (chip == 0))
        start(full, *[copy(mine, mine, sm.at[b, 3], rmq.at[b], plane[d], z) for d in range(15)])
        owe(full, m.at[pl.ds(0, 120)], sm.at[b, 3])
        short = deal_z & (chip != 0)

        @pl.when(short)
        def _():
            for d in range(15):
                start(chips[d] != 0, copy(mine, mine, sm.at[b, 3], rmq.at[b], plane[d], z))

        owe(short, m.at[pl.ds(0, 112)], sm.at[b, 3])
        if b == 3:
            start(source, copy(m, m, sm.at[b, 4], rms.at[b], sib, z))
            owe(source, m, sm.at[b, 4])

    def collect(b):
        m = msgs[b]
        kb = carrier(b)
        source = (r == kb) & (z == 0)
        carries = (k == kb) & jnp.logical_not(source)

        @pl.when(carries)
        def _():
            landed(m.at[pl.ds(0, 120)], rmq.at[b])
            copy(m, m, sm.at[b, 4], rms.at[b], sib, z)().start()

        owe(carries, m, sm.at[b, 4])
        has = (k == kb) | is_root if b < 3 else k == kb

        @pl.when(jnp.logical_not(has))
        def _():
            landed(m, rms.at[b])

    grow = lax.broadcasted_iota(jnp.int32, (256, 128), 0) + 256 * r

    def panel_rows(b, last):
        m = msgs[b]
        part = slice(128 * (b % 2), 128 * (b % 2) + 128)
        ts = split(m[:, 0:128])
        p = dot(ar[b // 2, :, part], ts, NT)
        gcol = lax.broadcasted_iota(jnp.int32, (256, 128), 1) + 128 * b
        pr[:, 128 * b : 128 * b + 128] = jnp.where(gcol <= grow, p, 0.0)
        ps = split(p)
        lefts = {h: split(left_of(b, h)) for h in range(b + 1, last)}
        for h in range(b + 1, last):
            hl = slice(128 * (h % 2), 128 * (h % 2) + 128)
            ar[h // 2, :, hl] = ar[h // 2, :, hl] - dot(ps, lefts[h], NN)
        return ts, ps, lefts

    def update(b):
        ts, ps, lefts = panel_rows(b, 4)
        rl = slice(128 * (b % 2), 128 * (b % 2) + 128)
        for j in range(4):
            q = split(dot(ts, ac[b // 2, j, rl, :], NN))
            for h in range(b + 1, 4):
                hl = slice(128 * (h % 2), 128 * (h % 2) + 128)
                ac[h // 2, j, hl, :] = ac[h // 2, j, hl, :] - dot(lefts[h], q, TN)
            sl = slice(256 * j, 256 * j + 256)
            acc[:, sl] = acc[:, sl] - dot(ps, q, NN)

    def step(b):
        @pl.when(r >= 2)
        def _():
            update(b)

    for b in range(4):
        @pl.when(is_root)
        def _():
            root_step(b)

        if b < 3:
            relay(b)
    relay(3)
    before = len(pending)
    pass_on()
    inputs_sent += pending[before:]
    collect(0)
    collect(1)
    collect(2)
    finish_inputs()
    step(0)
    step(1)
    step(2)
    collect(3)
    step(3)

    @pl.when(r == 0)
    def _():
        panel_rows(0, 2)
        panel_rows(1, 2)
        pr[:, 256:512] = jnp.zeros((256, 256), F32)

    @pl.when(r == 1)
    def _():
        for b in range(4):
            panel_rows(b, 4)

    for j in range(4):
        keep = (r >= 2) & (8 * j + z >= 2)
        sl = slice(256 * j, 256 * j + 256)
        acc[:, sl] = jnp.where(keep, acc[:, sl], 0.0)
    outs = [pltpu.make_async_copy(acc.at[:, pl.ds(256 * j, 256)], tr_ref.at[0, 0, :, j, 0, :], o_sem.at[j]) for j in range(4)]
    outs += [pltpu.make_async_copy(pr.at[:, pl.ds(256 * j, 256)], fac_ref.at[0, 0, :, j, :], o_sem.at[4 + j]) for j in range(2)]
    for q in outs:
        q.start()
    done = {id(e) for e in inputs_sent}
    drain([e for e in pending if id(e) not in done])
    for q in outs:
        q.wait()


def body(cov, noise):
    anywhere = pl.BlockSpec(memory_space=pl.ANY)
    dma = pltpu.SemaphoreType.DMA
    return pl.pallas_call(
        kernel,
        in_specs=[anywhere, anywhere],
        out_specs=[anywhere, anywhere],
        out_shape=[
            jax.ShapeDtypeStruct((1, 1, 256, 2, 256), F32),
            jax.ShapeDtypeStruct((1, 1, 256, 4, 1, 256), F32),
        ],
        scratch_shapes=[
            pltpu.SMEM((1,), F32),
            dma,
            pltpu.VMEM((512, 512), F32),
            pltpu.VMEM((2, 256, 256), F32),
            pltpu.VMEM((2, 4, 256, 256), F32),
            pltpu.VMEM((256, 1024), F32),
            pltpu.VMEM((256, 512), F32),
        ]
        + [pltpu.VMEM((128, w), F32) for w in WIDTHS]
        + [
            dma((4,)), dma((4,)), dma, dma((6,)),
            dma((2, 4, CHUNKS)), dma, dma, dma, dma,
            dma((2,)), dma((2,)), dma((2,)), dma((2,)), dma((2,)), dma,
            dma((4,)), dma((4,)), dma((4,)), dma((4,)), dma((4, 5)),
        ],
        compiler_params=pltpu.CompilerParams(collective_id=0, has_side_effects=True, vmem_limit_bytes=40 * 2**20),
    )(noise.reshape(1), cov)


def solution(mesh):
    return jax.shard_map(
        body,
        mesh=mesh,
        in_specs=(P(None, "row", None, None, "col", None), P()),
        out_specs=(P(None, "row", None, None, None), P(None, "row", None, None, "col", None)),
        check_vma=False,
    )
```

```python
import jax
import jax.numpy as jnp
from jax import lax
from jax.experimental import pallas as pl
from jax.experimental.pallas import tpu as pltpu
from jax.sharding import PartitionSpec as P

F32 = jnp.float32
NN = ((1,), (0,))
TN = ((0,), (0,))
NT = ((1,), (1,))
MESH = pl.DeviceIdType.MESH
CHUNKS = 4
WIDTHS = (512, 384, 256, 128)
FAR_FIRST = (10, 9, 11, 6, 14, 2, 8, 5, 7, 13, 15, 1, 3, 4, 12)


def split(a):
    hi = a.astype(jnp.bfloat16)
    return hi, (a - hi.astype(F32)).astype(jnp.bfloat16)


def dot(a, b, dims):
    a = a if isinstance(a, tuple) else split(a)
    b = b if isinstance(b, tuple) else split(b)

    def one(i, j):
        return lax.dot_general(a[i], b[j], (dims, ((), ())), preferred_element_type=F32)

    return one(0, 0) + (one(0, 1) + one(1, 0))


def lanes(v, q):
    return jnp.broadcast_to(v[:, q : q + 1], (8, 128))


def sublanes(v, j):
    return jnp.broadcast_to(v[j : j + 1, :], (8, 128))


def factor_inverse_64(tile, group=16):
    count = 8
    per = group // 8
    sub = lax.broadcasted_iota(jnp.int32, (8, 128), 0)
    lane = lax.broadcasted_iota(jnp.int32, (8, 128), 1)
    rows = []
    for h in range(count):
        left = jnp.concatenate([tile[8 * h : 8 * h + 8, :], jnp.zeros((8, 64), F32)], axis=1)
        rows.append(jnp.where(lane < 64, left, (lane - 64 == sub + 8 * h).astype(F32)))
    out = [None] * count
    for g in range(64 // group):
        first = g * per
        col = [[lanes(rows[first + a], group * g + j) for a in range(per)] for j in range(group)]
        later = range(first + per, count)
        mult = {h: [lanes(rows[h], group * g + j) for j in range(group)] for h in later}
        z = [rows[first + a] for a in range(per)]
        w = [jnp.zeros((8, 128), F32) for _ in range(per)]
        pivot = sublanes(col[0][0], 0)
        for j in range(group):
            a0, s0 = j // 8, j % 8
            here = sub == s0
            inv = 1.0 / pivot
            root = lax.rsqrt(pivot)
            if j + 1 < group:
                a1, s1 = (j + 1) // 8, (j + 1) % 8
                cross = sublanes(col[j][a1], s1) * sublanes(col[j + 1][a0], s0)
                pivot = sublanes(col[j + 1][a1], s1) - cross * inv
            line = sublanes(z[a0], s0)
            w[a0] = jnp.where(here, line * root, w[a0])
            line = line * inv
            for a in range(per):
                t = z[a] - col[j][a] * line
                z[a] = jnp.where(here, line, t) if a == a0 else t
            for k in range(j + 1, group):
                m = sublanes(col[k][a0], s0) * inv
                for a in range(per):
                    t = col[k][a] - col[j][a] * m
                    col[k][a] = jnp.where(here, m, t) if a == a0 else t
        for a in range(per):
            out[first + a] = w[a]
        zb = [sublanes(z[j // 8], j % 8) for j in range(group)]
        for h in later:
            t = [mult[h][j] * zb[j] for j in range(group)]
            while len(t) > 1:
                t = [t[i] + t[i + 1] for i in range(0, len(t), 2)]
            rows[h] = rows[h] - t[0]
    return jnp.concatenate(out, axis=0)[:, 64:]


def factor_inverse_128(tile, t1=None):
    if t1 is None:
        t1 = factor_inverse_64(tile[:64, :64])
    t1s = split(t1)
    u = split(dot(t1s, tile[:64, 64:], NN))
    rest = tile[64:, 64:] - dot(u, u, TN)
    x = dot(u, t1s, TN)
    t2 = factor_inverse_64(rest)
    y = -dot(t2, x, NN)
    top = jnp.concatenate([t1, jnp.zeros((64, 64), F32)], axis=1)
    return jnp.concatenate([top, jnp.concatenate([y, t2], axis=1)], axis=0)


def eye(n):
    return lax.broadcasted_iota(jnp.int32, (n, n), 0) == lax.broadcasted_iota(jnp.int32, (n, n), 1)


def kernel(
    noise_hbm, cov_ref, fac_ref, tr_ref,
    noise_ref, l_n, s_ref, ar, ac, acc, pr, m0, m1, m2, m3,
    l_a, l_c, l_r, o_sem,
    rc, sc1, sc2, sc3, scs,
    rr, ro, sr1, sr2, rs, ss,
    rmr, rmo, rmq, rms, sm,
):
    r = lax.axis_index("row")
    z = lax.axis_index("col")
    k = lax.rem(r, 2)
    chip = r // 2
    x = lax.rem(chip, 4)
    y = chip // 4
    u = jnp.where(k == 0, x, y)
    v = jnp.where(k == 0, y, x)

    def row_of(uu, vv):
        xx = jnp.where(k == 0, uu, vv)
        yy = jnp.where(k == 0, vv, uu)
        return (yy * 4 + xx) * 2 + k

    sib = r + 1 - 2 * k
    us = [lax.rem(u + d, 4) for d in (1, 2, 3)]
    vs = [lax.rem(v + d, 4) for d in (1, 2, 3)]
    zs = [lax.rem(z + d, 8) for d in range(1, 8)]
    u_row = [row_of(t, v) for t in us]
    v_row = [row_of(u, t) for t in vs]
    chips = [lax.rem(chip + d, 16) for d in range(1, 16)]
    plane = [2 * t + k for t in chips]
    msgs = (m0, m1, m2, m3)
    head = (u == 0) & (v == 0)
    is_root = (r == 0) & (z == 0)
    helper = (r == 1) & (z == 0)
    gives = (r == 1) & (z < 2)
    pending = []

    def copy(src, dst, send, recv, row, col):
        def make():
            return pltpu.make_async_remote_copy(
                src_ref=src, dst_ref=dst, send_sem=send, recv_sem=recv, device_id=(row, col), device_id_type=MESH
            )
        return make

    def start(cond, *makes):
        if cond is None:
            for make in makes:
                make().start()
        else:
            @pl.when(cond)
            def _():
                for make in makes:
                    make().start()

    def owe(cond, ref, sem):
        pending.append((cond, ref, sem))

    def landed(ref, sem):
        pltpu.make_async_copy(ref, ref, sem).wait()

    def when(cond, fn):
        pl.when(cond)(fn)

    loads_a = [pltpu.make_async_copy(cov_ref.at[0, 0, :, j, 0, :], acc.at[:, pl.ds(256 * j, 256)], l_a.at[j]) for j in range(4)]
    loads_c = [pltpu.make_async_copy(cov_ref.at[0, 0, :, j, 0, :], ac.at[k, j], l_c.at[j]) for j in range(4)]
    load_r = pltpu.make_async_copy(cov_ref.at[0, 0, :, 0, 0, :], ar.at[jnp.minimum(z, 1)], l_r)

    @pl.when(z < 2)
    def _():
        load_r.start()

    @pl.when(head)
    def _():
        for q in loads_c:
            q.start()

    for q in loads_a:
        q.start()
    load_n = pltpu.make_async_copy(noise_hbm, noise_ref, l_n)
    load_n.start()

    barrier = pltpu.get_barrier_semaphore()
    for t in plane + [sib]:
        pl.semaphore_signal(barrier, 1, device_id=(t, z), device_id_type=MESH)
    for t in zs:
        pl.semaphore_signal(barrier, 1, device_id=(r, t), device_id_type=MESH)

    @pl.when((r == 1) & (z == 1))
    def _():
        pl.semaphore_signal(barrier, 1, device_id=(0, 0), device_id_type=MESH)

    @pl.when(is_root)
    def _():
        pl.semaphore_signal(barrier, 1, device_id=(1, 1), device_id_type=MESH)

    load_n.wait()
    noise = noise_ref[0]

    @pl.when(z < 2)
    def _():
        load_r.wait()

    @pl.when((r == 0) & (z != 1))
    def _():
        ar[1] = jnp.zeros((256, 256), F32)

    @pl.when(is_root)
    def _():
        s_ref[0:256, 0:256] = ar[0] + jnp.where(eye(256), noise, 0.0)
        m0[0:64, 0:64] = factor_inverse_64(s_ref[0:64, 0:64])

    pl.semaphore_wait(barrier, 23 + jnp.where(((r == 1) & (z == 1)) | is_root, 1, 0))

    zc = jnp.minimum(z, 1)
    start(gives, copy(ar.at[zc], s_ref.at[pl.ds(256, 256), pl.ds(256 * zc, 256)], ss, rs.at[zc], 0, 0))
    owe(gives, ar.at[zc], ss)

    owners = (z == 0, (z == 1) & (r != 0))
    relays = (z != 0, (z != 1) & (r != 0))
    for s in range(2):
        makes = []
        for d in range(7):
            to = (s + d + 1) % 8
            part = ar.at[s, pl.ds(32 * to, 32)]
            makes.append(copy(part, part, sr1.at[s], ro.at[s], r, to))
        start(owners[s], *makes)
        owe(owners[s], ar.at[s, pl.ds(0, 224)], sr1.at[s])

    @pl.when(head)
    def _():
        for q in loads_c:
            q.wait()

    rows = 256 // CHUNKS

    def piece(half, j, ch):
        return ac.at[half, j, pl.ds(rows * ch, rows)]

    off_head = jnp.logical_not(head)
    for ch in range(CHUNKS):
        makes = [copy(piece(k, j, ch), piece(k, j, ch), sc1, rc.at[k, j, ch], row_of(j, 0), z) for j in (2, 1, 3)]
        start(head, *makes, copy(piece(k, 0, ch), piece(k, 0, ch), sc1, rc.at[k, 0, ch], row_of(0, 2), z))
    owe(head, ac.at[k], sc1)
    deals = (v == 0) & (u != 0)
    again = (v == 2) & (u == 0)
    skips = (v == 0) & (u != 0)
    for s in range(2):
        part = ar.at[s, pl.ds(32 * z, 32)]

        @pl.when(relays[s])
        def _():
            landed(part, ro.at[s])
            for d in range(7):
                start(zs[d] != s, copy(part, part, sr2.at[s], rr.at[s], r, zs[d]))

        owe(relays[s], ar.at[s, pl.ds(0, 192)], sr2.at[s])
        first = ar.at[s, pl.ds(32 * s, 32)]
        start(owners[s], *[copy(first, first, sr2.at[s], rr.at[s], r, (s + d + 1) % 8) for d in range(7)])
        owe(owners[s], ar.at[s, pl.ds(0, 224)], sr2.at[s])

    for ch in range(CHUNKS):
        mine = piece(k, u, ch)

        @pl.when(off_head)
        def _():
            landed(mine, rc.at[k, u, ch])

        start(deals, *[copy(mine, mine, sc2, rc.at[k, u, ch], v_row[d], z) for d in (1, 0, 2)])
        start(again, *[copy(mine, mine, sc2, rc.at[k, u, ch], row_of(0, t), z) for t in (1, 3)])
        for d in (1, 0, 2):
            start((v != 0) | (us[d] != 0), copy(mine, mine, sc3, rc.at[k, u, ch], u_row[d], z))
        start(None, copy(mine, mine, scs, rc.at[k, u, ch], sib, z))
    owe(deals, ac.at[k, pl.ds(0, 3)], sc2)
    owe(again, ac.at[k, pl.ds(0, 2)], sc2)
    owe(skips, ac.at[k, pl.ds(0, 2)], sc3)
    owe(jnp.logical_not(skips), ac.at[k, pl.ds(0, 3)], sc3)

    def pass_on():
        for ch in range(CHUNKS):
            for d in range(3):
                got = piece(k, us[d], ch)

                @pl.when(jnp.logical_not(head))
                def _():
                    landed(got, rc.at[k, us[d], ch])

                start(None, copy(got, got, scs, rc.at[k, us[d], ch], sib, z))
        owe(None, ac.at[k], scs)

    def drain(which):
        for cond, ref, sem in which:
            if cond is None:
                landed(ref, sem)
            else:
                pl.when(cond)(lambda ref=ref, sem=sem: landed(ref, sem))

    def finish_inputs():
        drain(inputs_sent)
        for ch in range(CHUNKS):
            for j in range(4):
                landed(piece(1 - k, j, ch), rc.at[1 - k, j, ch])
        for s in range(2):
            @pl.when(relays[s])
            def _():
                landed(ar.at[s, pl.ds(0, 224)], rr.at[s])

        for q in loads_a:
            q.wait()
        for j in range(4):
            extra = jnp.where((r // 8 == j) & (lax.rem(r, 8) == z), noise, 0.0)
            sl = slice(256 * j, 256 * j + 256)
            acc[:, sl] = acc[:, sl] + jnp.where(eye(256), extra, 0.0)
        for s in range(2):
            extra = jnp.where(r == s, noise, 0.0)
            ar[s] = ar[s] + jnp.where(eye(256), extra, 0.0)

    def left_of(b, h):
        return msgs[b][:, 128 * (h - b) : 128 * (h - b) + 128]

    def root_step(b):
        o = 128 * b
        if b == 0:
            m0[:, 0:128] = factor_inverse_128(s_ref[0:128, 0:128], m0[0:64, 0:64])
            landed(s_ref.at[pl.ds(256, 256), pl.ds(0, 256)], rs.at[0])
            s_ref[0:256, 256:512] = s_ref[256:512, 0:256].T
        else:
            c = b - 1
            if c == 0:
                landed(s_ref.at[pl.ds(256, 256), pl.ds(256, 256)], rs.at[1])
                s_ref[256:512, 256:512] = s_ref[256:512, 256:512] + jnp.where(eye(256), noise, 0.0)
            lefts = {h: split(left_of(c, h)) for h in range(b, 4)}
            tile = s_ref[o : o + 128, o : o + 128] - dot(lefts[b], lefts[b], TN)
            msgs[b][:, 0:128] = factor_inverse_128(tile)
            for h in range(b, 4):
                hl = slice(128 * h, 128 * h + 128)
                for w in range(max(h, b + 1), 4):
                    wl = slice(128 * w, 128 * w + 128)
                    s_ref[hl, wl] = s_ref[hl, wl] - dot(lefts[h], lefts[w], TN)
        if b < 3:
            msgs[b][:, 128:] = dot(msgs[b][:, 0:128], s_ref[o : o + 128, o + 128 :], NN)

    inputs_sent = list(pending)

    def share(b, q):
        return msgs[b].at[pl.ds(pl.multiple_of(8 * q, 8), 8)]

    def carrier(b):
        return 0 if b == 3 else 1

    def relay(b):
        m = msgs[b]
        kb = carrier(b)
        source = (r == kb) & (z == 0)
        carries = k == kb
        if b < 3:
            start(is_root, copy(m, m, sm.at[b, 0], rmr.at[b], 1, 0))
            owe(is_root, m, sm.at[b, 0])

            @pl.when(helper)
            def _():
                landed(m, rmr.at[b])

        start(source, *[copy(share(b, q), share(b, q), sm.at[b, 1], rmo.at[b], 2 * q + kb, 0) for q in FAR_FIRST])
        owe(source, m.at[pl.ds(0, 120)], sm.at[b, 1])
        mine = share(b, chip)

        @pl.when(carries & jnp.logical_not(source))
        def _():
            landed(mine, rmo.at[b])

        deal_z = carries & (z == 0)
        start(deal_z, *[copy(mine, mine, sm.at[b, 2], rmo.at[b], r, zs[d]) for d in range(7)])
        owe(deal_z, m.at[pl.ds(0, 56)], sm.at[b, 2])
        full = carries & ((z != 0) | (chip == 0))
        start(full, *[copy(mine, mine, sm.at[b, 3], rmq.at[b], plane[d], z) for d in range(15)])
        owe(full, m.at[pl.ds(0, 120)], sm.at[b, 3])
        short = deal_z & (chip != 0)

        @pl.when(short)
        def _():
            for d in range(15):
                start(chips[d] != 0, copy(mine, mine, sm.at[b, 3], rmq.at[b], plane[d], z))

        owe(short, m.at[pl.ds(0, 112)], sm.at[b, 3])
        if b == 3:
            start(source, copy(m, m, sm.at[b, 4], rms.at[b], sib, z))
            owe(source, m, sm.at[b, 4])

    def collect(b):
        m = msgs[b]
        kb = carrier(b)
        source = (r == kb) & (z == 0)
        carries = (k == kb) & jnp.logical_not(source)

        @pl.when(carries)
        def _():
            landed(m.at[pl.ds(0, 120)], rmq.at[b])
            copy(m, m, sm.at[b, 4], rms.at[b], sib, z)().start()

        owe(carries, m, sm.at[b, 4])
        has = (k == kb) | is_root if b < 3 else k == kb

        @pl.when(jnp.logical_not(has))
        def _():
            landed(m, rms.at[b])

    outs = [pltpu.make_async_copy(acc.at[:, pl.ds(256 * j, 256)], tr_ref.at[0, 0, :, j, 0, :], o_sem.at[j]) for j in range(4)]
    outs += [pltpu.make_async_copy(pr.at[:, pl.ds(256 * j, 256)], fac_ref.at[0, 0, :, j, :], o_sem.at[4 + j]) for j in range(2)]
    grow = lax.broadcasted_iota(jnp.int32, (256, 128), 0) + 256 * r

    def panel_rows(b, last):
        m = msgs[b]
        part = slice(128 * (b % 2), 128 * (b % 2) + 128)
        ts = split(m[:, 0:128])
        p = dot(ar[b // 2, :, part], ts, NT)
        gcol = lax.broadcasted_iota(jnp.int32, (256, 128), 1) + 128 * b
        pr[:, 128 * b : 128 * b + 128] = jnp.where(gcol <= grow, p, 0.0)
        ps = split(p)
        lefts = {h: split(left_of(b, h)) for h in range(b + 1, last)}
        for h in range(b + 1, last):
            hl = slice(128 * (h % 2), 128 * (h % 2) + 128)
            ar[h // 2, :, hl] = ar[h // 2, :, hl] - dot(ps, lefts[h], NN)
        return ts, ps, lefts

    def update(b):
        ts, ps, lefts = panel_rows(b, 4)
        rl = slice(128 * (b % 2), 128 * (b % 2) + 128)
        for j in range(4):
            q = split(dot(ts, ac[b // 2, j, rl, :], NN))
            for h in range(b + 1, 4):
                hl = slice(128 * (h % 2), 128 * (h % 2) + 128)
                ac[h // 2, j, hl, :] = ac[h // 2, j, hl, :] - dot(lefts[h], q, TN)
            sl = slice(256 * j, 256 * j + 256)
            new = acc[:, sl] - dot(ps, q, NN)
            acc[:, sl] = new if b < 3 else jnp.where(8 * j + z >= 2, new, 0.0)
        if b == 3:
            for q in outs:
                q.start()

    def step(b):
        @pl.when(r >= 2)
        def _():
            update(b)

    for b in range(4):
        @pl.when(is_root)
        def _():
            root_step(b)

        if b < 3:
            relay(b)
    relay(3)
    before = len(pending)
    pass_on()
    inputs_sent += pending[before:]
    collect(0)
    collect(1)
    collect(2)
    finish_inputs()
    step(0)
    step(1)
    step(2)
    collect(3)
    step(3)

    @pl.when(r == 0)
    def _():
        panel_rows(0, 2)
        panel_rows(1, 2)
        pr[:, 256:512] = jnp.zeros((256, 256), F32)

    @pl.when(r == 1)
    def _():
        for b in range(4):
            panel_rows(b, 4)

    @pl.when(r < 2)
    def _():
        acc[...] = jnp.zeros((256, 1024), F32)
        for q in outs:
            q.start()

    done = {id(e) for e in inputs_sent}
    drain([e for e in pending if id(e) not in done])
    for q in outs:
        q.wait()


def body(cov, noise):
    anywhere = pl.BlockSpec(memory_space=pl.ANY)
    dma = pltpu.SemaphoreType.DMA
    return pl.pallas_call(
        kernel,
        in_specs=[anywhere, anywhere],
        out_specs=[anywhere, anywhere],
        out_shape=[
            jax.ShapeDtypeStruct((1, 1, 256, 2, 256), F32),
            jax.ShapeDtypeStruct((1, 1, 256, 4, 1, 256), F32),
        ],
        scratch_shapes=[
            pltpu.SMEM((1,), F32),
            dma,
            pltpu.VMEM((512, 512), F32),
            pltpu.VMEM((2, 256, 256), F32),
            pltpu.VMEM((2, 4, 256, 256), F32),
            pltpu.VMEM((256, 1024), F32),
            pltpu.VMEM((256, 512), F32),
        ]
        + [pltpu.VMEM((128, w), F32) for w in WIDTHS]
        + [
            dma((4,)), dma((4,)), dma, dma((6,)),
            dma((2, 4, CHUNKS)), dma, dma, dma, dma,
            dma((2,)), dma((2,)), dma((2,)), dma((2,)), dma((2,)), dma,
            dma((4,)), dma((4,)), dma((4,)), dma((4,)), dma((4, 5)),
        ],
        compiler_params=pltpu.CompilerParams(collective_id=0, has_side_effects=True, vmem_limit_bytes=40 * 2**20),
    )(noise.reshape(1), cov)


def solution(mesh):
    return jax.shard_map(
        body,
        mesh=mesh,
        in_specs=(P(None, "row", None, None, "col", None), P()),
        out_specs=(P(None, "row", None, None, None), P(None, "row", None, None, "col", None)),
        check_vma=False,
    )
```

```python
import jax
import jax.numpy as jnp
from jax import lax
from jax.experimental import pallas as pl
from jax.experimental.pallas import tpu as pltpu
from jax.sharding import PartitionSpec as P

F32 = jnp.float32
NN = ((1,), (0,))
TN = ((0,), (0,))
NT = ((1,), (1,))
MESH = pl.DeviceIdType.MESH
CHUNKS = 4
WIDTHS = (512, 384, 256, 128)
FAR_FIRST = (10, 9, 11, 6, 14, 2, 8, 5, 7, 13, 15, 1, 3, 4, 12)


def split(a):
    hi = a.astype(jnp.bfloat16)
    return hi, (a - hi.astype(F32)).astype(jnp.bfloat16)


def dot(a, b, dims):
    a = a if isinstance(a, tuple) else split(a)
    b = b if isinstance(b, tuple) else split(b)

    def one(i, j):
        return lax.dot_general(a[i], b[j], (dims, ((), ())), preferred_element_type=F32)

    return one(0, 0) + (one(0, 1) + one(1, 0))


def lanes(v, q):
    return jnp.broadcast_to(v[:, q : q + 1], (8, 128))


def sublanes(v, j):
    return jnp.broadcast_to(v[j : j + 1, :], (8, 128))


def factor_inverse_64(tile, group=16):
    count = 8
    per = group // 8
    sub = lax.broadcasted_iota(jnp.int32, (8, 128), 0)
    lane = lax.broadcasted_iota(jnp.int32, (8, 128), 1)
    rows = []
    for h in range(count):
        left = jnp.concatenate([tile[8 * h : 8 * h + 8, :], jnp.zeros((8, 64), F32)], axis=1)
        rows.append(jnp.where(lane < 64, left, (lane - 64 == sub + 8 * h).astype(F32)))
    out = [None] * count
    for g in range(64 // group):
        first = g * per
        col = [[lanes(rows[first + a], group * g + j) for a in range(per)] for j in range(group)]
        later = range(first + per, count)
        mult = {h: [lanes(rows[h], group * g + j) for j in range(group)] for h in later}
        z = [rows[first + a] for a in range(per)]
        w = [jnp.zeros((8, 128), F32) for _ in range(per)]
        pivot = sublanes(col[0][0], 0)
        for j in range(group):
            a0, s0 = j // 8, j % 8
            here = sub == s0
            inv = 1.0 / pivot
            root = lax.rsqrt(pivot)
            if j + 1 < group:
                a1, s1 = (j + 1) // 8, (j + 1) % 8
                cross = sublanes(col[j][a1], s1) * sublanes(col[j + 1][a0], s0)
                pivot = sublanes(col[j + 1][a1], s1) - cross * inv
            line = sublanes(z[a0], s0)
            w[a0] = jnp.where(here, line * root, w[a0])
            line = line * inv
            for a in range(per):
                t = z[a] - col[j][a] * line
                z[a] = jnp.where(here, line, t) if a == a0 else t
            for k in range(j + 1, group):
                m = sublanes(col[k][a0], s0) * inv
                for a in range(per):
                    t = col[k][a] - col[j][a] * m
                    col[k][a] = jnp.where(here, m, t) if a == a0 else t
        for a in range(per):
            out[first + a] = w[a]
        zb = [sublanes(z[j // 8], j % 8) for j in range(group)]
        for h in later:
            t = [mult[h][j] * zb[j] for j in range(group)]
            while len(t) > 1:
                t = [t[i] + t[i + 1] for i in range(0, len(t), 2)]
            rows[h] = rows[h] - t[0]
    return jnp.concatenate(out, axis=0)[:, 64:]


def factor_inverse_128(tile, t1=None):
    if t1 is None:
        t1 = factor_inverse_64(tile[:64, :64])
    t1s = split(t1)
    u = split(dot(t1s, tile[:64, 64:], NN))
    rest = tile[64:, 64:] - dot(u, u, TN)
    x = dot(u, t1s, TN)
    t2 = factor_inverse_64(rest)
    y = -dot(t2, x, NN)
    top = jnp.concatenate([t1, jnp.zeros((64, 64), F32)], axis=1)
    return jnp.concatenate([top, jnp.concatenate([y, t2], axis=1)], axis=0)


def eye(n):
    return lax.broadcasted_iota(jnp.int32, (n, n), 0) == lax.broadcasted_iota(jnp.int32, (n, n), 1)


def kernel(
    noise_hbm, cov_ref, fac_ref, tr_ref,
    noise_ref, l_n, s_ref, ar, ac, acc, pr, m0, m1, m2, m3,
    l_a, l_c, l_r, o_sem,
    rc, sc1, sc2, sc3, scs,
    rr, ro, sr1, sr2, rs, ss,
    rmr, rmo, rmq, rms, sm,
):
    r = lax.axis_index("row")
    z = lax.axis_index("col")
    k = lax.rem(r, 2)
    chip = r // 2
    x = lax.rem(chip, 4)
    y = chip // 4
    u = jnp.where(k == 0, x, y)
    v = jnp.where(k == 0, y, x)

    def row_of(uu, vv):
        xx = jnp.where(k == 0, uu, vv)
        yy = jnp.where(k == 0, vv, uu)
        return (yy * 4 + xx) * 2 + k

    sib = r + 1 - 2 * k
    us = [lax.rem(u + d, 4) for d in (1, 2, 3)]
    vs = [lax.rem(v + d, 4) for d in (1, 2, 3)]
    zs = [lax.rem(z + d, 8) for d in range(1, 8)]
    u_row = [row_of(t, v) for t in us]
    v_row = [row_of(u, t) for t in vs]
    chips = [lax.rem(chip + d, 16) for d in range(1, 16)]
    plane = [2 * t + k for t in chips]
    msgs = (m0, m1, m2, m3)
    head = (u == 0) & (v == 0)
    is_root = (r == 0) & (z == 0)
    helper = (r == 1) & (z == 0)
    gives = (r == 1) & (z < 2)
    pending = []

    def copy(src, dst, send, recv, row, col):
        def make():
            return pltpu.make_async_remote_copy(
                src_ref=src, dst_ref=dst, send_sem=send, recv_sem=recv, device_id=(row, col), device_id_type=MESH
            )
        return make

    def start(cond, *makes):
        if cond is None:
            for make in makes:
                make().start()
        else:
            @pl.when(cond)
            def _():
                for make in makes:
                    make().start()

    def owe(cond, ref, sem):
        pending.append((cond, ref, sem))

    def landed(ref, sem):
        pltpu.make_async_copy(ref, ref, sem).wait()

    def when(cond, fn):
        pl.when(cond)(fn)

    loads_a = [pltpu.make_async_copy(cov_ref.at[0, 0, :, j, 0, :], acc.at[:, pl.ds(256 * j, 256)], l_a.at[j]) for j in range(4)]
    loads_c = [pltpu.make_async_copy(cov_ref.at[0, 0, :, j, 0, :], ac.at[k, j], l_c.at[j]) for j in range(4)]
    load_r = pltpu.make_async_copy(cov_ref.at[0, 0, :, 0, 0, :], ar.at[jnp.minimum(z, 1)], l_r)

    @pl.when(z < 2)
    def _():
        load_r.start()

    @pl.when(head)
    def _():
        for q in loads_c:
            q.start()

    for q in loads_a:
        q.start()
    load_n = pltpu.make_async_copy(noise_hbm, noise_ref, l_n)
    load_n.start()

    barrier = pltpu.get_barrier_semaphore()
    for t in plane + [sib]:
        pl.semaphore_signal(barrier, 1, device_id=(t, z), device_id_type=MESH)
    for t in zs:
        pl.semaphore_signal(barrier, 1, device_id=(r, t), device_id_type=MESH)

    @pl.when((r == 1) & (z == 1))
    def _():
        pl.semaphore_signal(barrier, 1, device_id=(0, 0), device_id_type=MESH)

    @pl.when(is_root)
    def _():
        pl.semaphore_signal(barrier, 1, device_id=(1, 1), device_id_type=MESH)

    load_n.wait()
    noise = noise_ref[0]

    @pl.when(z < 2)
    def _():
        load_r.wait()

    @pl.when((r == 0) & (z != 1))
    def _():
        ar[1] = jnp.zeros((256, 256), F32)

    @pl.when(is_root)
    def _():
        s_ref[0:256, 0:256] = ar[0] + jnp.where(eye(256), noise, 0.0)
        m0[0:64, 0:64] = factor_inverse_64(s_ref[0:64, 0:64])

    pl.semaphore_wait(barrier, 23 + jnp.where(((r == 1) & (z == 1)) | is_root, 1, 0))

    zc = jnp.minimum(z, 1)
    start(gives, copy(ar.at[zc], s_ref.at[pl.ds(256, 256), pl.ds(256 * zc, 256)], ss, rs.at[zc], 0, 0))
    owe(gives, ar.at[zc], ss)

    owners = (z == 0, (z == 1) & (r != 0))
    relays = (z != 0, (z != 1) & (r != 0))
    for s in range(2):
        makes = []
        for d in range(7):
            to = (s + d + 1) % 8
            part = ar.at[s, pl.ds(32 * to, 32)]
            makes.append(copy(part, part, sr1.at[s], ro.at[s], r, to))
        start(owners[s], *makes)
        owe(owners[s], ar.at[s, pl.ds(0, 224)], sr1.at[s])

    @pl.when(head)
    def _():
        for q in loads_c:
            q.wait()

    rows = 256 // CHUNKS

    def piece(half, j, ch):
        return ac.at[half, j, pl.ds(rows * ch, rows)]

    off_head = jnp.logical_not(head)
    for ch in range(CHUNKS):
        makes = [copy(piece(k, j, ch), piece(k, j, ch), sc1, rc.at[k, j, ch], row_of(j, 0), z) for j in (2, 1, 3)]
        start(head, *makes, copy(piece(k, 0, ch), piece(k, 0, ch), sc1, rc.at[k, 0, ch], row_of(0, 2), z))
    owe(head, ac.at[k], sc1)
    deals = (v == 0) & (u != 0)
    again = (v == 2) & (u == 0)
    skips = (v == 0) & (u != 0)
    for s in range(2):
        part = ar.at[s, pl.ds(32 * z, 32)]

        @pl.when(relays[s])
        def _():
            landed(part, ro.at[s])
            for d in range(7):
                start(zs[d] != s, copy(part, part, sr2.at[s], rr.at[s], r, zs[d]))

        owe(relays[s], ar.at[s, pl.ds(0, 192)], sr2.at[s])
        first = ar.at[s, pl.ds(32 * s, 32)]
        start(owners[s], *[copy(first, first, sr2.at[s], rr.at[s], r, (s + d + 1) % 8) for d in range(7)])
        owe(owners[s], ar.at[s, pl.ds(0, 224)], sr2.at[s])

    for ch in range(CHUNKS):
        mine = piece(k, u, ch)

        @pl.when(off_head)
        def _():
            landed(mine, rc.at[k, u, ch])

        start(deals, *[copy(mine, mine, sc2, rc.at[k, u, ch], v_row[d], z) for d in (1, 0, 2)])
        start(again, *[copy(mine, mine, sc2, rc.at[k, u, ch], row_of(0, t), z) for t in (1, 3)])
        for d in (1, 0, 2):
            start((v != 0) | (us[d] != 0), copy(mine, mine, sc3, rc.at[k, u, ch], u_row[d], z))
        start(None, copy(mine, mine, scs, rc.at[k, u, ch], sib, z))
    owe(deals, ac.at[k, pl.ds(0, 3)], sc2)
    owe(again, ac.at[k, pl.ds(0, 2)], sc2)
    owe(skips, ac.at[k, pl.ds(0, 2)], sc3)
    owe(jnp.logical_not(skips), ac.at[k, pl.ds(0, 3)], sc3)

    def pass_on():
        for ch in range(CHUNKS):
            for d in range(3):
                got = piece(k, us[d], ch)

                @pl.when(jnp.logical_not(head))
                def _():
                    landed(got, rc.at[k, us[d], ch])

                start(None, copy(got, got, scs, rc.at[k, us[d], ch], sib, z))
        owe(None, ac.at[k], scs)

    def drain(which):
        for cond, ref, sem in which:
            if cond is None:
                landed(ref, sem)
            else:
                pl.when(cond)(lambda ref=ref, sem=sem: landed(ref, sem))

    def finish_inputs():
        drain(inputs_sent)
        for ch in range(CHUNKS):
            for j in range(4):
                landed(piece(1 - k, j, ch), rc.at[1 - k, j, ch])
        for s in range(2):
            @pl.when(relays[s])
            def _():
                landed(ar.at[s, pl.ds(0, 224)], rr.at[s])

        for q in loads_a:
            q.wait()
        for j in range(4):
            extra = jnp.where((r // 8 == j) & (lax.rem(r, 8) == z), noise, 0.0)
            sl = slice(256 * j, 256 * j + 256)
            acc[:, sl] = acc[:, sl] + jnp.where(eye(256), extra, 0.0)
        for s in range(2):
            extra = jnp.where(r == s, noise, 0.0)
            ar[s] = ar[s] + jnp.where(eye(256), extra, 0.0)

    def left_of(b, h):
        return msgs[b][:, 128 * (h - b) : 128 * (h - b) + 128]

    def root_step(b):
        o = 128 * b
        if b == 0:
            m0[:, 0:128] = factor_inverse_128(s_ref[0:128, 0:128], m0[0:64, 0:64])
            landed(s_ref.at[pl.ds(256, 256), pl.ds(0, 256)], rs.at[0])
            s_ref[0:256, 256:512] = s_ref[256:512, 0:256].T
        else:
            c = b - 1
            if c == 0:
                landed(s_ref.at[pl.ds(256, 256), pl.ds(256, 256)], rs.at[1])
                s_ref[256:512, 256:512] = s_ref[256:512, 256:512] + jnp.where(eye(256), noise, 0.0)
            lefts = {h: split(left_of(c, h)) for h in range(b, 4)}
            tile = s_ref[o : o + 128, o : o + 128] - dot(lefts[b], lefts[b], TN)
            msgs[b][:, 0:128] = factor_inverse_128(tile)
            for h in range(b, 4):
                hl = slice(128 * h, 128 * h + 128)
                for w in range(max(h, b + 1), 4):
                    wl = slice(128 * w, 128 * w + 128)
                    s_ref[hl, wl] = s_ref[hl, wl] - dot(lefts[h], lefts[w], TN)
        if b < 3:
            msgs[b][:, 128:] = dot(msgs[b][:, 0:128], s_ref[o : o + 128, o + 128 :], NN)

    inputs_sent = list(pending)

    def share(b, q):
        return msgs[b].at[pl.ds(pl.multiple_of(8 * q, 8), 8)]

    def carrier(b):
        return 0 if b == 3 else 1

    def relay(b):
        m = msgs[b]
        kb = carrier(b)
        source = (r == kb) & (z == 0)
        carries = k == kb
        if b < 3:
            start(is_root, copy(m, m, sm.at[b, 0], rmr.at[b], 1, 0))
            owe(is_root, m, sm.at[b, 0])

            @pl.when(helper)
            def _():
                landed(m, rmr.at[b])

        start(source, *[copy(share(b, q), share(b, q), sm.at[b, 1], rmo.at[b], 2 * q + kb, 0) for q in FAR_FIRST])
        owe(source, m.at[pl.ds(0, 120)], sm.at[b, 1])
        mine = share(b, chip)

        @pl.when(carries & jnp.logical_not(source))
        def _():
            landed(mine, rmo.at[b])

        deal_z = carries & (z == 0)
        start(deal_z, *[copy(mine, mine, sm.at[b, 2], rmo.at[b], r, zs[d]) for d in range(7)])
        owe(deal_z, m.at[pl.ds(0, 56)], sm.at[b, 2])
        full = carries & ((z != 0) | (chip == 0))
        start(full, *[copy(mine, mine, sm.at[b, 3], rmq.at[b], plane[d], z) for d in range(15)])
        owe(full, m.at[pl.ds(0, 120)], sm.at[b, 3])
        short = deal_z & (chip != 0)

        @pl.when(short)
        def _():
            for d in range(15):
                start(chips[d] != 0, copy(mine, mine, sm.at[b, 3], rmq.at[b], plane[d], z))

        owe(short, m.at[pl.ds(0, 112)], sm.at[b, 3])
        if b == 3:
            start(source, copy(m, m, sm.at[b, 4], rms.at[b], sib, z))
            owe(source, m, sm.at[b, 4])

    def collect(b):
        m = msgs[b]
        kb = carrier(b)
        source = (r == kb) & (z == 0)
        carries = (k == kb) & jnp.logical_not(source)

        @pl.when(carries)
        def _():
            landed(m.at[pl.ds(0, 120)], rmq.at[b])
            copy(m, m, sm.at[b, 4], rms.at[b], sib, z)().start()

        owe(carries, m, sm.at[b, 4])
        has = (k == kb) | is_root if b < 3 else k == kb

        @pl.when(jnp.logical_not(has))
        def _():
            landed(m, rms.at[b])

    outs = [pltpu.make_async_copy(acc.at[:, pl.ds(256 * j, 256)], tr_ref.at[0, 0, :, j, 0, :], o_sem.at[j]) for j in range(4)]
    outs += [pltpu.make_async_copy(pr.at[:, pl.ds(256 * j, 256)], fac_ref.at[0, 0, :, j, :], o_sem.at[4 + j]) for j in range(2)]
    grow = lax.broadcasted_iota(jnp.int32, (256, 128), 0) + 256 * r

    def panel_rows(b, last):
        m = msgs[b]
        part = slice(128 * (b % 2), 128 * (b % 2) + 128)
        ts = split(m[:, 0:128])
        p = dot(ar[b // 2, :, part], ts, NT)
        gcol = lax.broadcasted_iota(jnp.int32, (256, 128), 1) + 128 * b
        pr[:, 128 * b : 128 * b + 128] = jnp.where(gcol <= grow, p, 0.0)
        ps = split(p)
        lefts = {h: split(left_of(b, h)) for h in range(b + 1, last)}
        for h in range(b + 1, last):
            hl = slice(128 * (h % 2), 128 * (h % 2) + 128)
            ar[h // 2, :, hl] = ar[h // 2, :, hl] - dot(ps, lefts[h], NN)
        return ts, ps, lefts

    def update(b):
        ts, ps, lefts = panel_rows(b, 4)
        rl = slice(128 * (b % 2), 128 * (b % 2) + 128)
        for j in range(4):
            q = split(dot(ts, ac[b // 2, j, rl, :], NN))
            for h in range(b + 1, 4):
                hl = slice(128 * (h % 2), 128 * (h % 2) + 128)
                ac[h // 2, j, hl, :] = ac[h // 2, j, hl, :] - dot(lefts[h], q, TN)
            sl = slice(256 * j, 256 * j + 256)
            new = acc[:, sl] - dot(ps, q, NN)
            acc[:, sl] = new if b < 3 else jnp.where(8 * j + z >= 2, new, 0.0)
        if b == 3:
            for q in outs:
                q.start()

    def step(b):
        @pl.when(r >= 2)
        def _():
            update(b)

    for b in range(4):
        @pl.when(is_root)
        def _():
            root_step(b)

        if b < 3:
            relay(b)
    relay(3)
    before = len(pending)
    pass_on()
    inputs_sent += pending[before:]
    collect(0)
    collect(1)
    collect(2)
    finish_inputs()
    step(0)
    step(1)
    step(2)
    collect(3)
    step(3)

    @pl.when(r == 0)
    def _():
        panel_rows(0, 2)
        panel_rows(1, 2)
        pr[:, 256:512] = jnp.zeros((256, 256), F32)

    @pl.when(r == 1)
    def _():
        for b in range(4):
            panel_rows(b, 4)

    @pl.when(r < 2)
    def _():
        acc[...] = jnp.zeros((256, 1024), F32)
        for q in outs:
            q.start()

    done = {id(e) for e in inputs_sent}
    drain([e for e in pending if id(e) not in done])
    for q in outs:
        q.wait()


def body(cov, noise):
    anywhere = pl.BlockSpec(memory_space=pl.ANY)
    dma = pltpu.SemaphoreType.DMA
    return pl.pallas_call(
        kernel,
        in_specs=[anywhere, pl.BlockSpec(memory_space=pltpu.HBM)],
        out_specs=[anywhere, anywhere],
        out_shape=[
            jax.ShapeDtypeStruct((1, 1, 256, 2, 256), F32),
            jax.ShapeDtypeStruct((1, 1, 256, 4, 1, 256), F32),
        ],
        scratch_shapes=[
            pltpu.SMEM((1,), F32),
            dma,
            pltpu.VMEM((512, 512), F32),
            pltpu.VMEM((2, 256, 256), F32),
            pltpu.VMEM((2, 4, 256, 256), F32),
            pltpu.VMEM((256, 1024), F32),
            pltpu.VMEM((256, 512), F32),
        ]
        + [pltpu.VMEM((128, w), F32) for w in WIDTHS]
        + [
            dma((4,)), dma((4,)), dma, dma((6,)),
            dma((2, 4, CHUNKS)), dma, dma, dma, dma,
            dma((2,)), dma((2,)), dma((2,)), dma((2,)), dma((2,)), dma,
            dma((4,)), dma((4,)), dma((4,)), dma((4,)), dma((4, 5)),
        ],
        compiler_params=pltpu.CompilerParams(collective_id=0, has_side_effects=True, vmem_limit_bytes=40 * 2**20),
    )(noise.reshape(1), cov)


def solution(mesh):
    return jax.shard_map(
        body,
        mesh=mesh,
        in_specs=(P(None, "row", None, None, "col", None), P()),
        out_specs=(P(None, "row", None, None, None), P(None, "row", None, None, "col", None)),
        check_vma=False,
    )
```
